768 devices in a mesh: table: 64 (over y, x, core), rep: 12 (over z).
Axes of the slice: x: 4, y: 8, z: 12, core: 2. Of those that a mesh axis runs over, the one named last changes fastest.
Arguments:
- item_rows: float32 [196608, 64], P('table')
- row_accum: float32 [196608], P('table'), may hold values from 1e-06 to 0.0001
- w_query: float32 [64, 64], replicated
- w_hidden: float32 [192, 200], replicated, may hold values from -0.4375 to 0.4375
- w_logit: float32 [200], replicated, may hold values from -0.4375 to 0.4375
- wanted_rows: int32 [768, 64, 48], P(('table', 'rep')), may hold values from 0 to 3071, as said below
- behaviour_slots: int32 [6144, 1024], P(('table', 'rep')), may hold values from 0 to 3071, as said below
- target_slots: int32 [6144], P(('table', 'rep')), may hold values from 0 to 3071, as said below
- seq_lengths: int32 [6144], P(('table', 'rep')), may hold values from 32 to 1024
- clicks: int32 [6144], P(('table', 'rep')), may hold values 0 or 1
- fake_flags: int32 [6144], P(('table', 'rep')), may hold values 0 or 1
Outputs:
- new_rows: float32 [196608, 64], P('table')
- new_accum: float32 [196608], P('table')
- grad_query: float32 [64, 64], replicated
- grad_hidden: float32 [192, 200], replicated
- grad_logit: float32 [200], replicated
The draws below stay inside these ranges and needn't reach their ends.
Inputs may be any that keep to these rules, and one draw needn't show every extreme that they name: `wanted_rows`: the 48 rows that one device asks of one owner are distinct, and entry k of such a list lies in rows k * (64) to (k + 1) * 64 - 1. `behaviour_slots`: slot s refers to entry s % 48 of the device's list for owner s // 48. `target_slots`: a slot as in behaviour_slots.
All inputs are finite; a program needn't handle non-finite values. No bound on the sum of `clicks` or of `fake_flags` on one device may be relied on, other than what follows from the above.
Results may differ from the reference program's by a relative error of at most 0.00035.
Values sent between devices are 32-bit elements; how exact they have to be, the bound alone decides.
A program may use at most 32 MiB of HBM per device.

```python
import math
import jax
import jax.numpy as jnp
from jax import lax

E = 64
HID = 200
USERS_DEV = 8
SEQ = 1024
CAP = 48
ROWS_DEV = 3072
ROWS = 196608
USERS = 6144
N_TABLE = 64
N_REP = 12


def shared_users(key):
    key_a, key_b, key_c, key_d, key_e, key_f = jax.random.split(key, 6)
    slot_count = N_TABLE * CAP
    slots = jax.random.randint(key_a, (USERS, SEQ), 0, slot_count, dtype=jnp.int32)
    slots = slots.at[::USERS_DEV, 0].set(slot_count - 1).at[::USERS_DEV, 1].set(0)
    factor = jax.random.randint(key_b, (USERS // USERS_DEV,), 1, 5, dtype=jnp.int32)
    factor = jnp.repeat(factor, USERS_DEV)
    base = jax.random.randint(key_c, (USERS,), max(SEQ // 32, 1), SEQ // 4 + 1, dtype=jnp.int32)
    lengths = jnp.minimum(base * factor, SEQ)
    lengths = lengths.at[::3 * USERS_DEV].set(SEQ)
    pick = jax.random.randint(key_d, (USERS,), 0, SEQ, dtype=jnp.int32) % lengths
    from_history = slots[jnp.arange(USERS, dtype=jnp.int32), pick]
    other = jax.random.randint(key_e, (USERS,), 0, slot_count, dtype=jnp.int32)
    coin = jax.random.randint(key_f, (USERS,), 0, 2, dtype=jnp.int32)
    targets = jnp.where(coin == 1, from_history, other)
    targets = targets.at[::USERS_DEV].set(slot_count - 1)
    return (slots, lengths, targets)


def draw_behaviour_slots(key, part):
    return shared_users(key)[0]


def draw_seq_lengths(key, part):
    return shared_users(key)[1]


def draw_target_slots(key, part):
    return shared_users(key)[2]


def draw_wanted_rows(key, part):
    key = jax.random.fold_in(key, 11)
    stride = ROWS_DEV // CAP
    offset = jax.random.randint(key, (N_TABLE * N_REP, N_TABLE, CAP), 0, stride, dtype=jnp.int32)
    offset = offset.at[:, :, 0].set(0).at[:, :, CAP - 1].set(stride - 1)
    return jnp.arange(CAP, dtype=jnp.int32) * stride + offset


def draw_item_rows(key, part):
    key = jax.random.fold_in(key, 12)
    key_a = jax.random.fold_in(key, 0)
    return jnp.clip(0.5 * jax.random.normal(key_a, (ROWS, E), jnp.float32), -4.0, 4.0)


def draw_w_query(key, part):
    key = jax.random.fold_in(key, 13)
    return jnp.clip(jax.random.normal(key, (E, E), jnp.float32), -4.0, 4.0) * E ** (-0.5)


def plant(entries, own_key, smallest, high):
    shape = entries.shape
    index_at = [jax.random.randint(jax.random.fold_in(own_key, axis), (), 0, shape[axis]) for axis in range(len(shape))]
    entries = entries.at[tuple(index_at)].set(smallest)
    longest = shape.index(max(shape))
    index_at[longest] = (index_at[longest] + 1) % shape[longest]
    return entries.at[tuple(index_at)].set(high)


def steps_of(stream_key, dims, cuts, least, high):
    def one(position, parts):
        draws = jax.random.uniform(jax.random.fold_in(jax.random.fold_in(stream_key, 6), position), (parts,), jnp.float32, least / len(cuts), high / len(cuts))
        return jnp.repeat(jnp.exp(draws), dims[position] // parts).reshape((-1,) + (1,) * (len(dims) - position - 1))

    factor_of = one(*cuts[0])
    for cut in cuts[1:]:
        factor_of = factor_of * one(*cut)
    return factor_of


def centred(own_key, extent, width, limit, kind=jnp.bfloat16):
    entries = width * jax.random.normal(own_key, extent, jnp.float32)
    return jnp.clip(entries, min=-limit, max=limit).astype(kind)


def setup_inputs(seed: int = 0) -> dict:
    key_of = jax.random.split(jax.random.key(seed), 12)
    return {
        "item_rows": draw_item_rows(jax.random.fold_in(key_of[11], 71), 0),
        "row_accum": jnp.clip(jnp.exp(math.log(0.0001) - 4.6051702 * jax.random.uniform(key_of[1], (ROWS,), jnp.float32) ** steps_of(key_of[1], (ROWS,), ((0, 64),), -0.2, 0.2)), 9.999999974752427e-07, 0.0001),
        "w_query": draw_w_query(jax.random.fold_in(key_of[11], 71), 0),
        "w_hidden": centred(key_of[3], (3 * E, HID), (3 * E) ** -0.5, 0.4375, jnp.float32),
        "w_logit": centred(key_of[4], (HID,), HID ** -0.5, 0.4375, jnp.float32),
        "wanted_rows": draw_wanted_rows(jax.random.fold_in(key_of[11], 71), 0),
        "behaviour_slots": draw_behaviour_slots(jax.random.fold_in(key_of[11], 71), 0),
        "target_slots": draw_target_slots(jax.random.fold_in(key_of[11], 71), 0),
        "seq_lengths": draw_seq_lengths(jax.random.fold_in(key_of[11], 71), 0),
        "clicks": plant((jax.random.randint(key_of[9], (USERS,), 0, 3) < 1).astype(jnp.int32), jax.random.fold_in(key_of[9], 1), 0, 1),
        "fake_flags": plant((jax.random.randint(key_of[10], (USERS,), 0, 2) < 1).astype(jnp.int32), jax.random.fold_in(key_of[10], 1), 0, 1),
    }


FAKE_WEIGHT = 0.3
LEARN_RATE = 0.1

def forward_loss(keys, target, w_query, w_hidden, w_logit, seq_lengths, clicks, fake_flags):
    highest = lax.Precision.HIGHEST
    query = jnp.dot(target, w_query, precision=highest)
    scores = jnp.einsum('use,ue->us', keys, query, precision=highest) * keys.shape[2] ** (-0.5)
    valid = jnp.arange(keys.shape[1], dtype=jnp.int32)[None, :] < seq_lengths[:, None]
    largest = lax.stop_gradient(lax.optimization_barrier(jnp.max(jnp.where(valid, scores, -1e+30), axis=1, keepdims=True)))
    raised = jnp.exp(jnp.where(valid, scores - largest, -1e+30))
    weights = raised / lax.optimization_barrier(jnp.sum(raised, axis=1, keepdims=True))
    pooled = jnp.einsum('us,use->ue', weights, keys, precision=highest)
    features = jnp.concatenate([pooled, target, pooled * target], axis=1)
    hidden = jax.nn.silu(jnp.dot(features, w_hidden, precision=highest))
    logit = jnp.dot(hidden, w_logit, precision=highest)
    labels_f = clicks.astype(logit.dtype)
    scale = jnp.where(clicks == 1, 1.0, jnp.where(fake_flags == 1, FAKE_WEIGHT, 1.0)).astype(logit.dtype)
    return jnp.sum(scale * (jax.nn.softplus(logit) - labels_f * logit))

def device_grads(slot_rows, slots, targets, seq_lengths, clicks, fake_flags, w_query, w_hidden, w_logit):
    keys = slot_rows[slots]
    target = slot_rows[targets]

    def local_loss(keys_in, target_in, query_in, hidden_in, logit_in):
        return forward_loss(keys_in, target_in, query_in, hidden_in, logit_in, seq_lengths, clicks, fake_flags)
    loss, pull = jax.vjp(local_loss, keys, target, w_query, w_hidden, w_logit)
    return pull(jnp.ones_like(loss))

def reference(item_rows, row_accum, w_query, w_hidden, w_logit, wanted_rows, behaviour_slots, target_slots, seq_lengths, clicks, fake_flags):
    devices = N_TABLE * N_REP
    slot_count = N_TABLE * CAP
    owner_base = jnp.repeat(jnp.arange(N_TABLE, dtype=jnp.int32) * ROWS_DEV, CAP)

    def visit(carry, packed):
        row_grad, acc_query, acc_hidden, acc_logit = carry
        wanted, slots, targets, lengths_d, clicks_d, flags_d = packed
        rows = (owner_base + wanted.reshape(-1)).astype(jnp.int32)
        slot_rows = item_rows[rows]
        key_grad, target_grad, d_query, d_hidden, d_logit = device_grads(slot_rows, slots, targets, lengths_d, clicks_d, flags_d, w_query, w_hidden, w_logit)
        key_grad = lax.optimization_barrier(key_grad.astype(jnp.bfloat16)).astype(jnp.float32)
        slot_grad = jax.ops.segment_sum(key_grad.reshape(-1, E), slots.reshape(-1), slot_count)
        slot_grad = slot_grad + jax.ops.segment_sum(target_grad, targets, slot_count)
        row_grad = row_grad.at[rows].add(slot_grad)
        return ((row_grad, acc_query + d_query, acc_hidden + d_hidden, acc_logit + d_logit), None)
    packed = (wanted_rows, behaviour_slots.reshape(devices, USERS_DEV, SEQ), target_slots.reshape(devices, USERS_DEV), seq_lengths.reshape(devices, USERS_DEV), clicks.reshape(devices, USERS_DEV), fake_flags.reshape(devices, USERS_DEV))
    start = (jnp.zeros(item_rows.shape, jnp.float32), jnp.zeros(w_query.shape, jnp.float32), jnp.zeros(w_hidden.shape, jnp.float32), jnp.zeros(w_logit.shape, jnp.float32))
    (row_grad, grad_query, grad_hidden, grad_logit), _ = lax.scan(visit, start, packed)
    new_accum = row_accum + lax.optimization_barrier(jnp.mean(row_grad * row_grad, axis=1))
    new_rows = item_rows - LEARN_RATE * row_grad / jnp.sqrt(new_accum)[:, None]
    return (new_rows, new_accum, grad_query, grad_hidden, grad_logit)
```

```python
import functools

import jax
import jax.numpy as jnp
from jax import lax
from jax.experimental import pallas as pl
from jax.experimental.pallas import tpu as pltpu
from jax.sharding import PartitionSpec as P

FAKE_WEIGHT = 0.3
LEARN_RATE = 0.1
MESH = pl.DeviceIdType.MESH
CORES, CHIPS_X = 2, 4
LANES = 128
E = 64
HID = 200
USERS = 8
PIECE = 24
F32, BF16 = jnp.float32, jnp.bfloat16


def iota(shape, dim):
    return lax.broadcasted_iota(jnp.int32, shape, dim)


def exact_dot(a, b, contract=((1,), (0,))):
    return lax.dot_general(
        a, b, (contract, ((), ())), precision=lax.Precision.HIGHEST, preferred_element_type=F32
    )


def bf16_dot(a, b, contract=((1,), (0,))):
    return lax.dot_general(a, b, (contract, ((), ())), preferred_element_type=F32)


def split3(x):
    high = x.astype(BF16)
    rest = x - high.astype(F32)
    middle = rest.astype(BF16)
    return high, middle, (rest - middle.astype(F32)).astype(BF16)


def column(ref):
    at = iota((USERS, 1), 0)
    out = jnp.zeros((USERS, 1), jnp.int32)
    for user in range(USERS):
        out = jnp.where(at == user, ref[user], out)
    return out


def place_of(slots, capacity):
    owner = lax.shift_right_logical(slots * 87382, 22)
    entry = slots - owner * capacity
    return owner * (capacity // 2) + lax.shift_right_logical(entry, 1), entry & 1


def sigmoid(x):
    return 1.0 / (1.0 + jnp.exp(-x))


def kernel(
    nt, nr, capacity,
    items, accum, w_query, w_hidden, w_logit, want, slots, targets, lengths, clicks, flags,
    out_rows, out_accum, out_query, out_hidden, out_logit,
    parts, asked_out, asked, onehot, looked, fetched, fetched_t, count, aimed, code_hi, code_lo,
    weight, dscore, cast, slot_grad, homed, index_t, named, sums_r, sums_l, got_r, got_l,
    weights, weights_z, weights_c, weights_x, weights_y, share,
    ask_sem, row_sem, grad_sem, wz_sem, wc_sem, wx_sem, wy_sem,
    rs_send_r, rs_recv_r, rs_send_l, rs_recv_l, ag_send_r, ag_recv_r, ag_send_l, ag_recv_l,
):
    me, rep = lax.axis_index("table"), lax.axis_index("rep")
    pairs = capacity // 2
    per_rep = pairs // nr
    columns = nt * pairs
    steps_r, steps_l = nr // 2, nr - 1 - nr // 2
    right, left = lax.rem(rep + 1, nr), lax.rem(rep + nr - 1, nr)

    def block(i):
        return pl.ds(pl.multiple_of(i * pairs, 8), pairs)

    def send(src, dst, sems, to):
        pltpu.make_async_remote_copy(
            src_ref=src, dst_ref=dst, send_sem=sems[0], recv_sem=sems[1], device_id=to, device_id_type=MESH
        ).start()

    def wait_bytes(ref, sem):
        pltpu.make_async_copy(ref, ref, sem).wait()

    barrier = pltpu.get_barrier_semaphore()

    @pl.loop(1, nt)
    def _(i):
        pl.semaphore_signal(barrier, inc=1, device_id={"table": lax.rem(me + i, nt)}, device_id_type=MESH)

    @pl.loop(1, nr)
    def _(i):
        pl.semaphore_signal(barrier, inc=1, device_id={"rep": lax.rem(rep + i, nr)}, device_id_type=MESH)

    wanted = jnp.concatenate([want[...], jnp.zeros((LANES - capacity, nt), jnp.int32)], axis=0)
    asked_out[...] = wanted.T.reshape(nt, 1, LANES)
    for p, part in enumerate(split3(items[...])):
        parts[p] = part
    pl.semaphore_wait(barrier, nt - 1 + nr - 1)

    pltpu.make_async_copy(asked_out.at[me], asked.at[me], ask_sem.at[1]).start()

    @pl.loop(1, nt)
    def _(i):
        to = lax.rem(me + i, nt)
        send(asked_out.at[to], asked.at[me], (ask_sem.at[0], ask_sem.at[1]), {"table": to})

    wait_bytes(asked, ask_sem.at[1])

    asked_t = jnp.concatenate([asked[...].reshape(nt, LANES), jnp.zeros((LANES - nt, LANES), jnp.int32)], axis=0).T
    first = iota((LANES, nt), 0)
    low_half = iota((E, LANES), 1) < E
    index_t[...] = asked_t.reshape(LANES, 1, LANES)

    @pl.loop(0, pairs)
    def _(k):
        at = first + k * LANES
        hot = (at == index_t[2 * k][:, 0:nt]) | (at == index_t[2 * k + 1][:, 0:nt])
        hot = hot.astype(F32).astype(BF16)
        onehot[k] = hot
        lhs = []
        for p in range(3):
            rows = parts[p, :, pl.ds(pl.multiple_of(k * LANES, LANES), LANES)]
            zero = jnp.zeros_like(rows)
            lhs += [jnp.where(low_half, rows, zero), jnp.where(low_half, zero, rows)]
        got = bf16_dot(jnp.concatenate(lhs, axis=0), hot)
        got = got[0:LANES] + got[LANES : 2 * LANES] + got[2 * LANES : 3 * LANES]
        looked[pl.ds(k, nt, stride=pairs), :] = got.T

    pltpu.make_async_copy(looked.at[block(me)], fetched.at[block(me)], row_sem.at[1]).start()

    @pl.loop(1, nt)
    def _(i):
        to = lax.rem(me + i, nt)
        send(looked.at[block(to)], fetched.at[block(me)], (row_sem.at[0], row_sem.at[1]), {"table": to})

    seq = slots.shape[1]
    place, half = place_of(slots[...], capacity)
    chunks = columns // LANES
    valid = iota((USERS, seq), 1) < column(lengths)
    code_hi[...] = jnp.where(valid, half * chunks + lax.shift_right_logical(place, 7), -1).reshape(USERS, 1, seq)
    code_lo[...] = (place & (LANES - 1)).reshape(USERS, 1, seq)

    @pl.loop(0, USERS)
    def _(user):
        hi = (iota((2 * chunks, seq), 0) == code_hi[user]).astype(F32).astype(BF16)
        lo = (iota((LANES, seq), 0) == code_lo[user]).astype(F32).astype(BF16)
        named[user] = bf16_dot(hi, lo, ((1,), (1,)))

    for h in range(2):
        for c in range(chunks):
            count[h * USERS : (h + 1) * USERS, c * LANES : (c + 1) * LANES] = named[:, h * chunks + c, :]

    target_place, target_half = place_of(column(targets), capacity)
    lane = iota((USERS, columns), 1)
    hit = lane == target_place
    for h in range(2):
        aimed[h * USERS : (h + 1) * USERS, :] = (hit & (target_half == h)).astype(F32)
    weights[...] = jnp.zeros_like(weights)

    wait_bytes(fetched, row_sem.at[1])

    @pl.loop(0, chunks)
    def _(c):
        at = pl.ds(pl.multiple_of(c * LANES, LANES), LANES)
        fetched_t[:, at] = fetched[at, :].T

    def fold(x):
        return x[0:USERS, 0:E] + x[USERS : 2 * USERS, E : 2 * E]

    def spread(x):
        zero = jnp.zeros_like(x)
        return jnp.concatenate(
            [jnp.concatenate([x, zero], axis=1), jnp.concatenate([zero, x], axis=1)], axis=0
        )

    def both(x):
        return jnp.concatenate([x, x], axis=0)

    rows = fetched[...]
    target = fold(exact_dot(aimed[...], rows))
    query = exact_dot(target, w_query[...]) * E ** (-0.5)
    scores = exact_dot(spread(query), fetched_t[...])
    times = count[...]
    present = times > 0.0
    scores = jnp.where(present, scores, -1e30)
    largest = jnp.max(scores, axis=1, keepdims=True)
    largest = both(jnp.maximum(largest[0:USERS], largest[USERS : 2 * USERS]))
    raised = jnp.where(present, jnp.exp(scores - largest), 0.0)
    total = jnp.sum(raised * times, axis=1, keepdims=True)
    total = both(total[0:USERS] + total[USERS : 2 * USERS])
    attention = raised / total
    weight[...] = attention
    pooled = fold(exact_dot(attention * times, rows))
    features = jnp.concatenate([pooled, target, pooled * target], axis=1)
    before = exact_dot(features, w_hidden[...])
    gate = sigmoid(before)
    hidden = before * gate
    logit = jnp.sum(hidden * w_logit[...], axis=1, keepdims=True)
    click = column(clicks)
    scale = jnp.where(click == 1, 1.0, jnp.where(column(flags) == 1, FAKE_WEIGHT, 1.0)).astype(F32)
    d_logit = scale * (sigmoid(logit) - click.astype(F32))
    d_before = d_logit * w_logit[...] * (gate + hidden * (1.0 - gate))
    weights[0 : 3 * E, 0:HID] = exact_dot(features.T, d_before)
    weights[4 * E : 4 * E + 1, 0:HID] = jnp.sum(hidden * d_logit, axis=0, keepdims=True)
    d_features = exact_dot(d_before, w_hidden[...], ((1,), (1,)))
    d_cross = d_features[:, 2 * E : 3 * E]
    d_pooled = d_features[:, 0:E] + d_cross * target
    d_target = d_features[:, E : 2 * E] + d_cross * pooled
    pull = exact_dot(spread(d_pooled), fetched_t[...])
    shift = jnp.sum(pooled * d_pooled, axis=1, keepdims=True)
    d_scores = attention * (pull - both(shift))
    dscore[...] = d_scores
    d_query = fold(exact_dot(d_scores * times, rows)) * E ** (-0.5)
    d_target = d_target + exact_dot(d_query, w_query[...], ((1,), (1,)))
    weights[3 * E : 4 * E, 0:E] = exact_dot(target.T, d_query)

    @pl.loop(1, nr)
    def _(i):
        to = lax.rem(rep + i, nr)
        piece = weights.at[pl.ds(pl.multiple_of(to * PIECE, 8), PIECE)]
        send(piece, weights_z.at[i - 1], (wz_sem.at[0], wz_sem.at[1]), {"rep": to})

    vectors = jnp.concatenate([d_pooled, query, d_target], axis=0)
    vectors = jnp.concatenate([vectors, jnp.zeros((3 * USERS, LANES - E), F32)], axis=1)
    vectors = jnp.concatenate([vectors, jnp.zeros((LANES - 3 * USERS, LANES), F32)], axis=0).T
    for i in range(3 * USERS):
        cast[i] = jnp.broadcast_to(vectors[0:E, i : i + 1], (E, LANES))

    @pl.loop(0, chunks)
    def _(c):
        at = pl.ds(pl.multiple_of(c * LANES, LANES), LANES)
        w_c, s_c, n_c, a_c = weight[:, at], dscore[:, at], count[:, at], aimed[:, at]
        halves = []
        for h in range(2):
            acc = jnp.zeros((E, LANES), F32)
            for u in range(USERS):
                row = slice(h * USERS + u, h * USERS + u + 1)
                key_grad = w_c[row] * cast[u] + s_c[row] * cast[USERS + u]
                key_grad = key_grad.astype(BF16).astype(F32)
                acc = acc + n_c[row] * key_grad + a_c[row] * cast[2 * USERS + u]
            halves.append(acc)
        slot_grad[at, :] = jnp.concatenate(halves, axis=0).T

    pltpu.make_async_copy(slot_grad.at[block(me)], homed.at[block(me)], grad_sem.at[1]).start()

    @pl.loop(1, nt)
    def _(i):
        to = lax.rem(me + i, nt)
        send(slot_grad.at[block(to)], homed.at[block(me)], (grad_sem.at[0], grad_sem.at[1]), {"table": to})

    wait_bytes(weights_z, wz_sem.at[1])
    piece = weights[pl.ds(pl.multiple_of(rep * PIECE, 8), PIECE), :]
    for i in range(nr - 1):
        piece = piece + weights_z[i]
    core = lax.rem(me, CORES)
    chip_x = lax.rem(lax.div(me, CORES), CHIPS_X)
    chip_y = lax.div(me, CORES * CHIPS_X)
    chips_y = nt // (CORES * CHIPS_X)

    def add_up(ref, count_of):
        out = ref[0]
        for i in range(1, count_of):
            out = out + ref[i]
        return out

    wait_bytes(homed, grad_sem.at[1])

    def send_cores():
        weights_c[core] = piece
        send(weights_c.at[core], weights_c.at[core], (wc_sem.at[0], wc_sem.at[1]), {"table": me + 1 - 2 * core})

    def send_x():
        wait_bytes(weights_c.at[0], wc_sem.at[1])
        weights_x[chip_x] = add_up(weights_c, CORES)

        @pl.loop(1, CHIPS_X)
        def _(i):
            to = lax.rem(chip_x + i, CHIPS_X)
            send(weights_x.at[chip_x], weights_x.at[chip_x], (wx_sem.at[0], wx_sem.at[1]),
                 {"table": (chip_y * CHIPS_X + to) * CORES + core})

    def send_y():
        wait_bytes(weights_x.at[pl.ds(0, CHIPS_X - 1)], wx_sem.at[1])
        weights_y[chip_y] = add_up(weights_x, CHIPS_X)

        @pl.loop(1, chips_y)
        def _(i):
            to = lax.rem(chip_y + i, chips_y)
            send(weights_y.at[chip_y], weights_y.at[chip_y], (wy_sem.at[0], wy_sem.at[1]),
                 {"table": (to * CHIPS_X + chip_x) * CORES + core})

    def own(dest, k):
        at = dest * per_rep + k
        parts_of = split3(homed[pl.ds(at, nt, stride=pairs), :])
        got = bf16_dot(onehot[at], jnp.concatenate(parts_of, axis=1))
        got = got[:, 0:LANES] + got[:, LANES : 2 * LANES] + got[:, 2 * LANES : 3 * LANES]
        return jnp.where(low_half, got[0:E], got[E : 2 * E])

    send_cores()
    for step in range(steps_r):
        for k in range(per_rep):
            dest = lax.rem(rep + steps_r - step, nr)
            value = own(dest, k)
            if step:
                wait_bytes(got_r.at[step - 1, k], rs_recv_r.at[step - 1, k])
                value = value + got_r[step - 1, k]
            sums_r[step, k] = value
            send(sums_r.at[step, k], got_r.at[step, k], (rs_send_r.at[step, k], rs_recv_r.at[step, k]), {"rep": right})
            if step < steps_l:
                dest = lax.rem(rep + nr - steps_l + step, nr)
                value = own(dest, k)
                if step:
                    wait_bytes(got_l.at[step - 1, k], rs_recv_l.at[step - 1, k])
                    value = value + got_l[step - 1, k]
                sums_l[step, k] = value
                send(sums_l.at[step, k], got_l.at[step, k], (rs_send_l.at[step, k], rs_recv_l.at[step, k]), {"rep": left})
        if step == 1:
            send_x()
        if step == 3:
            send_y()
    gradient = []
    for k in range(per_rep):
        value = own(rep, k)
        wait_bytes(got_l.at[steps_l - 1, k], rs_recv_l.at[steps_l - 1, k])
        value = value + got_l[steps_l - 1, k]
        wait_bytes(got_r.at[steps_r - 1, k], rs_recv_r.at[steps_r - 1, k])
        gradient.append(value + got_r[steps_r - 1, k])

    turned = jnp.concatenate(gradient, axis=0).T
    even, odd = turned[0:E], turned[E : 2 * E]
    blocks = [
        jnp.where(low_half, even, pltpu.roll(odd, E, 1)),
        jnp.where(low_half, pltpu.roll(even, E, 1), odd),
    ]
    for k in range(per_rep):
        at = rep * per_rep + k
        span = slice(k * LANES, (k + 1) * LANES)
        grads = blocks[k]
        new_accum = accum[at] + jnp.sum(grads * grads, axis=0, keepdims=True) * (1.0 / E)
        old = items[:, pl.ds(pl.multiple_of(at * LANES, LANES), LANES)]
        share[rep, 0:E, span] = old - LEARN_RATE * grads / jnp.sqrt(new_accum)
        share[rep, E : E + 8, span] = jnp.broadcast_to(new_accum, (8, LANES))
    wait_bytes(weights_y.at[pl.ds(0, chips_y - 1)], wy_sem.at[1])
    share[rep, E + 8 : E + 8 + PIECE, :] = add_up(weights_y, chips_y)

    cut = (E + 8 + PIECE) // 2
    spans = [pl.ds(0, cut), pl.ds(cut, cut)]

    def place(r):
        for k in range(per_rep):
            span = slice(k * LANES, (k + 1) * LANES)
            at = r * per_rep + k
            out_rows[:, pl.ds(pl.multiple_of(at * LANES, LANES), LANES)] = share[r, 0:E, span]
            out_accum[at] = share[r, E : E + 1, span]

    for step in range(steps_r):
        for k in range(2):
            source = lax.rem(rep + nr - step, nr)
            if step:
                wait_bytes(share.at[source, spans[k]], ag_recv_r.at[step - 1, k])
            part = share.at[source, spans[k]]
            send(part, part, (ag_send_r.at[step, k], ag_recv_r.at[step, k]), {"rep": right})
            if step < steps_l:
                source = lax.rem(rep + step, nr)
                if step:
                    wait_bytes(share.at[source, spans[k]], ag_recv_l.at[step - 1, k])
                part = share.at[source, spans[k]]
                send(part, part, (ag_send_l.at[step, k], ag_recv_l.at[step, k]), {"rep": left})
        place(lax.rem(rep + nr - step, nr))
        if 0 < step < steps_l:
            place(lax.rem(rep + step, nr))
    for k in range(2):
        source = lax.rem(rep + steps_l, nr)
        wait_bytes(share.at[source, spans[k]], ag_recv_l.at[steps_l - 1, k])
        source = lax.rem(rep + nr - steps_r, nr)
        wait_bytes(share.at[source, spans[k]], ag_recv_r.at[steps_r - 1, k])
    place(lax.rem(rep + steps_l, nr))
    place(lax.rem(rep + nr - steps_r, nr))

    flat = share[:, E + 8 : E + 8 + PIECE, :].reshape(nr * PIECE, 2 * LANES)
    out_hidden[...] = flat[0 : 3 * E, 0:HID]
    out_query[...] = flat[3 * E : 4 * E, 0:E]
    out_logit[...] = flat[4 * E : 4 * E + 1, 0:HID]

    wait_bytes(asked.at[pl.ds(0, nt - 1)], ask_sem.at[0])
    wait_bytes(looked.at[pl.ds(0, (nt - 1) * pairs)], row_sem.at[0])
    wait_bytes(slot_grad.at[pl.ds(0, (nt - 1) * pairs)], grad_sem.at[0])
    wait_bytes(weights_z, wz_sem.at[0])
    wait_bytes(weights_c.at[0], wc_sem.at[0])
    wait_bytes(weights_x.at[pl.ds(0, CHIPS_X - 1)], wx_sem.at[0])
    wait_bytes(weights_y.at[pl.ds(0, chips_y - 1)], wy_sem.at[0])
    for step in range(steps_r):
        for k in range(per_rep):
            wait_bytes(sums_r.at[step, k], rs_send_r.at[step, k])
            if step < steps_l:
                wait_bytes(sums_l.at[step, k], rs_send_l.at[step, k])
        for k in range(2):
            wait_bytes(share.at[0, spans[k]], ag_send_r.at[step, k])
            if step < steps_l:
                wait_bytes(share.at[0, spans[k]], ag_send_l.at[step, k])


def local(
    nt, nr, item_rows, row_accum, w_query, w_hidden, w_logit, wanted_rows, behaviour_slots,
    target_slots, seq_lengths, clicks, fake_flags,
):
    rows = item_rows.shape[0]
    capacity = wanted_rows.shape[2]
    pairs = capacity // 2
    columns = nt * pairs
    seq = behaviour_slots.shape[1]
    steps_r, steps_l = nr // 2, nr - 1 - nr // 2
    per_rep = pairs // nr
    vmem = pl.BlockSpec(memory_space=pltpu.VMEM)
    smem = pl.BlockSpec(memory_space=pltpu.SMEM)
    dma = pltpu.SemaphoreType.DMA
    wide = 2 * LANES
    scratch = [
        pltpu.VMEM((3, E, rows), BF16),
        pltpu.VMEM((nt, 1, LANES), jnp.int32),
        pltpu.VMEM((nt, 1, LANES), jnp.int32),
        pltpu.VMEM((pairs, LANES, nt), BF16),
        pltpu.VMEM((columns, LANES), F32),
        pltpu.VMEM((columns, LANES), F32),
        pltpu.VMEM((LANES, columns), F32),
        pltpu.VMEM((2 * USERS, columns), F32),
        pltpu.VMEM((2 * USERS, columns), F32),
        pltpu.VMEM((USERS, 1, seq), jnp.int32),
        pltpu.VMEM((USERS, 1, seq), jnp.int32),
        pltpu.VMEM((2 * USERS, columns), F32),
        pltpu.VMEM((2 * USERS, columns), F32),
        pltpu.VMEM((3 * USERS, E, LANES), F32),
        pltpu.VMEM((columns, LANES), F32),
        pltpu.VMEM((columns, LANES), F32),
        pltpu.VMEM((LANES, 1, LANES), jnp.int32),
        pltpu.VMEM((USERS, 2 * columns // LANES, LANES), F32),
        pltpu.VMEM((steps_r, per_rep, E, LANES), F32),
        pltpu.VMEM((steps_l, per_rep, E, LANES), F32),
        pltpu.VMEM((steps_r, per_rep, E, LANES), F32),
        pltpu.VMEM((steps_l, per_rep, E, LANES), F32),
        pltpu.VMEM((nr * PIECE, wide), F32),
        pltpu.VMEM((nr - 1, PIECE, wide), F32),
        pltpu.VMEM((CORES, PIECE, wide), F32),
        pltpu.VMEM((CHIPS_X, PIECE, wide), F32),
        pltpu.VMEM((nt // (CORES * CHIPS_X), PIECE, wide), F32),
        pltpu.VMEM((nr, E + 8 + PIECE, wide), F32),
        dma((2,)), dma((2,)), dma((2,)), dma((2,)), dma((2,)), dma((2,)), dma((2,)),
        dma((steps_r, per_rep)), dma((steps_r, per_rep)), dma((steps_l, per_rep)), dma((steps_l, per_rep)),
        dma((steps_r, 2)), dma((steps_r, 2)), dma((steps_l, 2)), dma((steps_l, 2)),
    ]
    new_rows, new_accum, grad_query, grad_hidden, grad_logit = pl.pallas_call(
        functools.partial(kernel, nt, nr, capacity),
        out_shape=(
            jax.ShapeDtypeStruct((E, rows), F32),
            jax.ShapeDtypeStruct((rows // LANES, 1, LANES), F32),
            jax.ShapeDtypeStruct((E, E), F32),
            jax.ShapeDtypeStruct((3 * E, HID), F32),
            jax.ShapeDtypeStruct((1, HID), F32),
        ),
        in_specs=[vmem] * 7 + [smem] * 4,
        out_specs=[vmem] * 5,
        scratch_shapes=scratch,
        compiler_params=pltpu.CompilerParams(
            collective_id=0, has_side_effects=True, vmem_limit_bytes=48 * 1024 * 1024
        ),
    )(
        item_rows.T,
        row_accum.reshape(rows // LANES, 1, LANES),
        w_query,
        w_hidden,
        w_logit.reshape(1, HID),
        wanted_rows[0].T,
        behaviour_slots,
        target_slots,
        seq_lengths,
        clicks,
        fake_flags,
    )
    return (new_rows.T, new_accum.reshape(rows), grad_query, grad_hidden, grad_logit.reshape(HID))


def solution(mesh):
    in_specs = (
        P("table", None),
        P("table"),
        P(),
        P(),
        P(),
        P(("table", "rep"), None, None),
        P(("table", "rep"), None),
        P(("table", "rep")),
        P(("table", "rep")),
        P(("table", "rep")),
        P(("table", "rep")),
    )
    out_specs = (P("table", None), P("table"), P(), P(), P())
    return jax.shard_map(
        functools.partial(local, mesh.shape["table"], mesh.shape["rep"]),
        mesh=mesh, in_specs=in_specs, out_specs=out_specs, check_vma=False,
    )
```

```python
import functools

import jax
import jax.numpy as jnp
from jax import lax
from jax.experimental import pallas as pl
from jax.experimental.pallas import tpu as pltpu
from jax.sharding import PartitionSpec as P

FAKE_WEIGHT = 0.3
LEARN_RATE = 0.1
MESH = pl.DeviceIdType.MESH
CORES, CHIPS_X = 2, 4
LANES = 128
E = 64
HID = 200
USERS = 8
PIECE = 16
VMEM = 65000000
F32, BF16 = jnp.float32, jnp.bfloat16


def iota(shape, dim):
    return lax.broadcasted_iota(jnp.int32, shape, dim)


def exact_dot(a, b, contract=((1,), (0,))):
    return lax.dot_general(
        a, b, (contract, ((), ())), precision=lax.Precision.HIGHEST, preferred_element_type=F32
    )


def bf16_dot(a, b, contract=((1,), (0,))):
    return lax.dot_general(a, b, (contract, ((), ())), preferred_element_type=F32)


def split3(x):
    high = x.astype(BF16)
    rest = x - high.astype(F32)
    middle = rest.astype(BF16)
    return high, middle, (rest - middle.astype(F32)).astype(BF16)


def column(ref):
    at = iota((USERS, 1), 0)
    out = jnp.zeros((USERS, 1), jnp.int32)
    for user in range(USERS):
        out = jnp.where(at == user, ref[user], out)
    return out


def place_of(slots, capacity):
    owner = lax.shift_right_logical(slots * 87382, 22)
    entry = slots - owner * capacity
    k = lax.shift_right_logical(entry, 1) & 1
    return owner * (capacity // 2) + k * (capacity // 4) + lax.shift_right_logical(entry, 2), entry & 1


def early_rows(pairs):
    return -(-(pairs // 2) // 8) * 8


def sigmoid(x):
    return 1.0 / (1.0 + jnp.exp(-x))


def kernel(
    nt, nr, capacity,
    items_hbm, accum_hbm, w_query_hbm, w_hidden_hbm, w_logit_hbm, want_hbm, slots_hbm,
    targets_hbm, lengths_hbm, clicks_hbm, flags_hbm,
    out_rows, out_accum, out_query, out_hidden, out_logit,
    items, accum, w_query, w_hidden, w_logit, want, slots, targets, lengths, clicks, flags,
    parts, asked_out, asked, onehot, looked, fetched, fetched_t, count, aimed, code_hi, code_lo,
    weight, dscore, cast, slot_grad, homed_a, homed_b, index_t, named, sums, got,
    weights, weights_z, weights_c, weights_x, weights_y, cuts, spread_out, joined, whole, share,
    in_sem, ask_sem, row_sem, grad_sem, wz_sem, wc_sem, wx_sem, wy_sem, ws_sem, wj_sem, rs_send, rs_recv, ag_send, ag_recv,
):
    me, rep = lax.axis_index("table"), lax.axis_index("rep")
    pairs = capacity // 2
    per_rep = pairs // nr
    columns = nt * pairs
    rows = items_hbm.shape[1]

    def at_rep(distance):
        return lax.rem(rep + nr + distance, nr)

    def block(i):
        return pl.ds(pl.multiple_of(i * pairs, 8), pairs)

    def send(src, dst, sems, to):
        pltpu.make_async_remote_copy(
            src_ref=src, dst_ref=dst, send_sem=sems[0], recv_sem=sems[1], device_id=to, device_id_type=MESH
        ).start()

    def wait_bytes(ref, sem):
        pltpu.make_async_copy(ref, ref, sem).wait()

    drains = []
    brought = [
        pltpu.make_async_copy(src, dst, in_sem.at[i])
        for i, (src, dst) in enumerate([
            (want_hbm, want), (items_hbm, items), (slots_hbm, slots), (lengths_hbm, lengths), (targets_hbm, targets),
            (clicks_hbm, clicks), (flags_hbm, flags), (accum_hbm, accum), (w_query_hbm, w_query),
            (w_hidden_hbm, w_hidden), (w_logit_hbm, w_logit),
        ])
    ]
    brought[0].start()
    core = lax.rem(me, CORES)
    chip_x = lax.rem(lax.div(me, CORES), CHIPS_X)
    chip_y = lax.div(me, CORES * CHIPS_X)
    row = CORES * CHIPS_X
    chips_y = nt // row

    def device(y, x, c):
        return (lax.rem(y, chips_y) * CHIPS_X + lax.rem(x, CHIPS_X)) * CORES + lax.rem(c, CORES)

    def partner(j):
        m = lax.rem(j, chips_y)
        n = lax.rem(lax.div(j, chips_y) + 1, row)
        down, step = lax.rem(m, 2), lax.div(m, 2)
        dy = (chips_y // 2 - step) * (1 - down) + lax.rem(chips_y // 2 + 1 + step, chips_y) * down
        return device(chip_y + dy, chip_x + lax.div(n, CORES), core + lax.rem(n, CORES))

    barrier = pltpu.get_barrier_semaphore()

    @pl.loop(1, nt)
    def _(i):
        pl.semaphore_signal(barrier, inc=1, device_id={"table": lax.rem(me + i, nt)}, device_id_type=MESH)

    @pl.loop(1, nr)
    def _(i):
        pl.semaphore_signal(barrier, inc=1, device_id={"rep": lax.rem(rep + i, nr)}, device_id_type=MESH)

    for copy in brought[1:]:
        copy.start()
    brought[0].wait()
    wanted = jnp.concatenate([want[...], jnp.zeros((LANES - capacity, nt), jnp.int32)], axis=0)
    asked_out[...] = wanted.T.reshape(nt, 1, LANES)
    pl.semaphore_wait(barrier, nt - 1 + nr - 1)

    pltpu.make_async_copy(asked_out.at[me], asked.at[me], ask_sem.at[1]).start()

    @pl.loop(1, nt)
    def _(i):
        to = lax.rem(me + i, nt)
        send(asked_out.at[to], asked.at[me], (ask_sem.at[0], ask_sem.at[1]), {"table": to})

    drains.append((asked.at[pl.ds(0, nt - 1)], ask_sem.at[0]))
    for copy in brought[1:]:
        copy.wait()
    low_half = iota((E, LANES), 1) < E
    wide_low = (iota((E, rows), 1) & (LANES - 1)) < E
    for p, part in enumerate(split3(items[...])):
        part = part.astype(F32)
        parts[p * LANES : p * LANES + E, :] = jnp.where(wide_low, part, 0.0).astype(BF16)
        parts[p * LANES + E : (p + 1) * LANES, :] = jnp.where(wide_low, 0.0, part).astype(BF16)

    seq = slots.shape[1]
    place, half = place_of(slots[...], capacity)
    chunks = columns // LANES
    valid = iota((USERS, seq), 1) < column(lengths)
    code_hi[...] = jnp.where(valid, half * chunks + lax.shift_right_logical(place, 7), -1).reshape(USERS, 1, seq)
    code_lo[...] = (place & (LANES - 1)).reshape(USERS, 1, seq)

    @pl.loop(0, USERS)
    def _(user):
        hi = (iota((2 * chunks, seq), 0) == code_hi[user]).astype(F32).astype(BF16)
        lo = (iota((LANES, seq), 0) == code_lo[user]).astype(F32).astype(BF16)
        named[user] = bf16_dot(hi, lo, ((1,), (1,)))

    for h in range(2):
        for c in range(chunks):
            count[h * USERS : (h + 1) * USERS, c * LANES : (c + 1) * LANES] = named[:, h * chunks + c, :]

    target_place, target_half = place_of(column(targets), capacity)
    lane = iota((USERS, columns), 1)
    hit = lane == target_place
    for h in range(2):
        aimed[h * USERS : (h + 1) * USERS, :] = (hit & (target_half == h)).astype(F32)
    weights[:, LANES : 2 * LANES] = jnp.zeros((3 * E, LANES), F32)

    wait_bytes(asked, ask_sem.at[1])

    asked_t = jnp.concatenate([asked[...].reshape(nt, LANES), jnp.zeros((LANES - nt, LANES), jnp.int32)], axis=0).T
    first = iota((LANES, nt), 0)
    index_t[...] = asked_t.reshape(LANES, 1, LANES)

    @pl.loop(0, pairs, unroll=8)
    def _(p):
        k = per_rep * p - (per_rep * nr - 1) * lax.div(p, nr)
        at = first + k * LANES
        hot = (at == index_t[2 * k][:, 0:nt]) | (at == index_t[2 * k + 1][:, 0:nt])
        hot = hot.astype(F32).astype(BF16)
        onehot[p] = hot
        found = bf16_dot(parts[:, pl.ds(pl.multiple_of(k * LANES, LANES), LANES)], hot)
        found = found[0:LANES] + found[LANES : 2 * LANES] + found[2 * LANES : 3 * LANES]
        looked[pl.ds(p, nt, stride=pairs), :] = found.T

    pltpu.make_async_copy(looked.at[block(me)], fetched.at[block(me)], row_sem.at[1]).start()

    @pl.loop(0, nt - 1)
    def _(j):
        to = partner(j)
        send(looked.at[block(to)], fetched.at[block(me)], (row_sem.at[0], row_sem.at[1]), {"table": to})

    drains.append((looked.at[pl.ds(0, (nt - 1) * pairs)], row_sem.at[0]))
    wait_bytes(fetched, row_sem.at[1])

    @pl.loop(0, chunks)
    def _(c):
        at = pl.ds(pl.multiple_of(c * LANES, LANES), LANES)
        fetched_t[:, at] = fetched[at, :].T

    def fold(x):
        return x[0:USERS, 0:E] + x[USERS : 2 * USERS, E : 2 * E]

    def spread(x):
        zero = jnp.zeros_like(x)
        return jnp.concatenate(
            [jnp.concatenate([x, zero], axis=1), jnp.concatenate([zero, x], axis=1)], axis=0
        )

    def both(x):
        return jnp.concatenate([x, x], axis=0)

    keys = fetched[...]
    target = fold(exact_dot(aimed[...], keys))
    query = exact_dot(target, w_query[...]) * E ** (-0.5)
    scores = exact_dot(spread(query), fetched_t[...])
    times = count[...]
    present = times > 0.0
    scores = jnp.where(present, scores, -1e30)
    largest = jnp.max(scores, axis=1, keepdims=True)
    largest = both(jnp.maximum(largest[0:USERS], largest[USERS : 2 * USERS]))
    raised = jnp.where(present, jnp.exp(scores - largest), 0.0)
    total = jnp.sum(raised * times, axis=1, keepdims=True)
    total = both(total[0:USERS] + total[USERS : 2 * USERS])
    attention = raised / total
    weight[...] = attention
    pooled = fold(exact_dot(attention * times, keys))
    features = jnp.concatenate([pooled, target, pooled * target], axis=1)
    before = exact_dot(features, w_hidden[...])
    gate = sigmoid(before)
    hidden = before * gate
    logit = jnp.sum(hidden * w_logit[...], axis=1, keepdims=True)
    click = column(clicks)
    scale = jnp.where(click == 1, 1.0, jnp.where(column(flags) == 1, FAKE_WEIGHT, 1.0)).astype(F32)
    d_logit = scale * (sigmoid(logit) - click.astype(F32))
    d_before = d_logit * w_logit[...] * (gate + hidden * (1.0 - gate))
    weights[:, 0:HID] = exact_dot(features.T, d_before)
    d_w_logit = jnp.sum(hidden * d_logit, axis=0, keepdims=True)
    d_features = exact_dot(d_before, w_hidden[...], ((1,), (1,)))
    d_cross = d_features[:, 2 * E : 3 * E]
    d_pooled = d_features[:, 0:E] + d_cross * target
    d_target = d_features[:, E : 2 * E] + d_cross * pooled
    pull = exact_dot(spread(d_pooled), fetched_t[...])
    shift = jnp.sum(pooled * d_pooled, axis=1, keepdims=True)
    d_scores = attention * (pull - both(shift))
    dscore[...] = d_scores
    d_query = fold(exact_dot(d_scores * times, keys)) * E ** (-0.5)
    d_target = d_target + exact_dot(d_query, w_query[...], ((1,), (1,)))
    d_w_query = exact_dot(target.T, d_query)
    spare = HID - LANES
    room = LANES - spare
    low = jnp.concatenate([d_w_query, jnp.zeros((E, LANES - E), F32)], axis=1)
    row_a = d_w_logit[:, 0:LANES]
    row_b = jnp.concatenate([d_w_logit[:, LANES:HID], jnp.zeros((1, room), F32)], axis=1)
    logit_rows = [
        pltpu.roll(row_a, spare, 1), pltpu.roll(row_a, spare - room, 1), pltpu.roll(row_a, spare + LANES - 2 * room, 1),
        pltpu.roll(row_b, spare, 1), pltpu.roll(row_b, spare - room, 1), jnp.zeros((E - 5, LANES), F32),
    ]
    extra = [pltpu.roll(low, spare, 1), pltpu.roll(low, spare - room, 1)] + logit_rows
    second = weights[:, LANES : 2 * LANES]
    free = iota((3 * E, LANES), 1) >= spare
    weights[:, LANES : 2 * LANES] = jnp.where(free, jnp.concatenate(extra, axis=0), second)

    @pl.loop(1, nr)
    def _(i):
        to = lax.rem(rep + i, nr)
        piece = weights.at[pl.ds(pl.multiple_of(to * PIECE, 8), PIECE)]
        send(piece, weights_z.at[i - 1], (wz_sem.at[0], wz_sem.at[1]), {"rep": to})

    drains.append((weights_z, wz_sem.at[0]))
    vectors = jnp.concatenate([d_pooled, query, d_target], axis=0)
    vectors = jnp.concatenate([vectors, jnp.zeros((3 * USERS, LANES - E), F32)], axis=1)
    vectors = jnp.concatenate([vectors, jnp.zeros((LANES - 3 * USERS, LANES), F32)], axis=0).T
    for i in range(3 * USERS):
        cast[i] = jnp.broadcast_to(vectors[0:E, i : i + 1], (E, LANES))

    def slot_grads(c):
        at = pl.ds(pl.multiple_of(c * LANES, LANES), LANES)
        w_c, s_c, n_c, a_c = weight[:, at], dscore[:, at], count[:, at], aimed[:, at]
        halves = []
        for h in range(2):
            acc = jnp.zeros((E, LANES), F32)
            for u in range(USERS):
                row = slice(h * USERS + u, h * USERS + u + 1)
                key_grad = w_c[row] * cast[u] + s_c[row] * cast[USERS + u]
                key_grad = key_grad.astype(BF16).astype(F32)
                acc = acc + n_c[row] * key_grad + a_c[row] * cast[2 * USERS + u]
            halves.append(acc)
        slot_grad[at, :] = jnp.concatenate(halves, axis=0).T

    groups = 4
    members, group_chunks = nt // groups, chunks // groups

    def send_grads(to, landing, first_row, count_of, sems):
        src = slot_grad.at[pl.ds(pl.multiple_of(to * pairs + first_row, 8), count_of)]
        dst = landing.at[pl.ds(pl.multiple_of(me * count_of, 8), count_of)]

        @pl.when(to != me)
        def _():
            send(src, dst, sems, {"table": to})

        @pl.when(to == me)
        def _():
            pltpu.make_async_copy(src, dst, sems[1]).start()

    early = early_rows(pairs)
    late = pairs - early
    for g in (2, 1, 3, 0):
        group = lax.rem(lax.div(me, members) + g, groups)

        @pl.loop(0, group_chunks)
        def _(i):
            slot_grads(group * group_chunks + i)

        @pl.loop(0, members)
        def _(i):
            to = group * members + lax.rem(me + i, members)
            send_grads(to, homed_a, 0, early, (grad_sem.at[0], grad_sem.at[1]))

    @pl.loop(0, nt)
    def _(j):
        send_grads(partner(j), homed_b, early, late, (grad_sem.at[2], grad_sem.at[3]))

    drains.append((homed_a.at[pl.ds(0, (nt - 1) * early)], grad_sem.at[0]))
    drains.append((homed_b.at[pl.ds(0, (nt - 1) * late)], grad_sem.at[2]))
    wait_bytes(weights_z, wz_sem.at[1])
    piece = weights[pl.ds(pl.multiple_of(rep * PIECE, 8), PIECE), :]
    for i in range(nr - 1):
        piece = piece + weights_z[i]
    def add_up(ref, count_of):
        out = ref[0]
        for i in range(1, count_of):
            out = out + ref[i]
        return out

    def send_cores():
        weights_c[core] = piece
        send(weights_c.at[core], weights_c.at[core], (wc_sem.at[0], wc_sem.at[1]), {"table": me + 1 - 2 * core})
        drains.append((weights_c.at[0], wc_sem.at[0]))

    def send_x():
        drains.append((weights_x.at[pl.ds(0, CHIPS_X - 1)], wx_sem.at[0]))
        wait_bytes(weights_c.at[0], wc_sem.at[1])
        weights_x[chip_x] = add_up(weights_c, CORES)

        @pl.loop(1, CHIPS_X)
        def _(i):
            to = lax.rem(chip_x + i, CHIPS_X)
            send(weights_x.at[chip_x], weights_x.at[chip_x], (wx_sem.at[0], wx_sem.at[1]),
                 {"table": (chip_y * CHIPS_X + to) * CORES + core})

    def send_y():
        drains.append((weights_y.at[pl.ds(0, chips_y - 1)], wy_sem.at[0]))
        wait_bytes(weights_x.at[pl.ds(0, CHIPS_X - 1)], wx_sem.at[1])
        weights_y[chip_y] = add_up(weights_x, CHIPS_X)

        @pl.loop(1, chips_y)
        def _(i):
            to = lax.rem(chip_y + i, chips_y)
            send(weights_y.at[chip_y], weights_y.at[chip_y], (wy_sem.at[0], wy_sem.at[1]),
                 {"table": (to * CHIPS_X + chip_x) * CORES + core})

    def send_weights():
        wait_bytes(weights_y.at[pl.ds(0, chips_y - 1)], wy_sem.at[1])
        total = add_up(weights_y, chips_y)
        for spot in range(row):
            cuts[spot] = total[spot * PIECE // row : (spot + 1) * PIECE // row]
        spread_out[rep] = cuts[lax.rem(me, row)]

        @pl.loop(1, nr)
        def _(i):
            to = lax.rem(rep + i, nr)
            send(spread_out.at[rep], spread_out.at[rep], (ws_sem.at[0], ws_sem.at[1]), {"rep": to})

        drains.append((spread_out.at[pl.ds(0, nr - 1)], ws_sem.at[0]))

    def share_weights():
        wait_bytes(spread_out.at[pl.ds(0, nr - 1)], ws_sem.at[1])
        spot = lax.rem(me, row)
        joined[spot] = spread_out[...]

        @pl.loop(1, row)
        def _(i):
            to = chip_y * row + lax.rem(spot + i, row)
            send(joined.at[spot], joined.at[spot], (wj_sem.at[0], wj_sem.at[1]), {"table": to})

        drains.append((joined.at[pl.ds(0, row - 1)], wj_sem.at[0]))

    def own(dest, k):
        at = k * nr + dest
        if k == 0:
            rows_of = homed_a[pl.ds(at, nt, stride=early), :]
        else:
            ahead = at < early
            in_a = homed_a[pl.ds(jnp.minimum(at, early - 1), nt, stride=early), :]
            in_b = homed_b[pl.ds(jnp.maximum(at - early, 0), nt, stride=late), :]
            rows_of = jnp.where(ahead, in_a, in_b)
        here = bf16_dot(onehot[at], jnp.concatenate(split3(rows_of), axis=1))
        here = here[:, 0:LANES] + here[:, LANES : 2 * LANES] + here[:, 2 * LANES : 3 * LANES]
        return jnp.where(low_half, here[0:E], here[E : 2 * E])

    plan = [
        (0, 6, 2, ()), (1, 5, 1, ()), (2, -5, -1, ()), (3, 3, 1, ()), (4, -3, -1, ()), (5, 1, 1, ()), (6, -1, -1, ()),
        (7, 4, 2, (0, 1)), (8, -4, -2, (2,)), (9, 2, 2, (7, 3)), (10, -2, -2, (8, 4)), (None, 0, 0, (5, 6, 9, 10)),
    ]
    sign = (1, -1)

    def sum_step(k, first_item, last_item):
        for slot, far, hop, terms in plan[first_item:last_item]:
            value = held[k].pop(0) if held[k] else own(at_rep(sign[k] * far), k)
            for term in terms:
                wait_bytes(got.at[term, k], rs_recv.at[term, k])
                value = value + got[term, k]
            if slot is None:
                return value
            sums[slot, k] = value
            send(sums.at[slot, k], got.at[slot, k], (rs_send.at[slot, k], rs_recv.at[slot, k]), {"rep": at_rep(sign[k] * hop)})
            drains.append((sums.at[slot, k], rs_send.at[slot, k]))

    held = ([], [])

    def adagrad(k, value):
        turned = jnp.concatenate([value, jnp.zeros_like(value)], axis=0).T
        grads = jnp.where(low_half, turned[0:E], pltpu.roll(turned[E : 2 * E], E, 1))
        at = rep * per_rep + k
        new_accum = accum[at] + jnp.sum(grads * grads, axis=0, keepdims=True) * (1.0 / E)
        old = items[:, pl.ds(pl.multiple_of(at * LANES, LANES), LANES)]
        share[rep, k, 0:E, :] = old - LEARN_RATE * grads / jnp.sqrt(new_accum)
        share[rep, k, E : E + 8, :] = jnp.broadcast_to(new_accum, (8, LANES))

    def place(r, k):
        at = r * per_rep + k
        out_rows[:, pl.ds(pl.multiple_of(at * LANES, LANES), LANES)] = share[r, k, 0:E, :]
        out_accum[at] = share[r, k, E : E + 1, :]

    def share_step(k, stage):
        for reach, way in ((6, sign[k]), (5, -sign[k])):
            side = 0 if reach == 6 else 6
            part = share.at[at_rep(-way * 2 * stage), k]
            if stage:
                wait_bytes(part, ag_recv.at[side + 2 * stage - 1, k])
            for hop in (2, 1):
                distance = 2 * stage + hop
                if distance <= reach:
                    at = side + distance - 1
                    send(part, part, (ag_send.at[at, k], ag_recv.at[at, k]), {"rep": at_rep(way * hop)})
                    drains.append((part, ag_send.at[at, k]))

    def place_step(k, distances):
        for distance, side in distances:
            way = sign[k] if side == 0 else -sign[k]
            source = at_rep(-way * distance)
            if distance % 2 or distance == 6:
                wait_bytes(share.at[source, k], ag_recv.at[side + distance - 1, k])
            place(source, k)

    send_cores()
    wait_bytes(homed_a, grad_sem.at[1])
    sum_step(0, 0, 7)
    sum_step(0, 7, 9)
    wait_bytes(homed_b, grad_sem.at[3])
    sum_step(1, 0, 7)
    send_x()
    sum_step(0, 9, 11)
    sum_step(1, 7, 9)
    send_y()
    adagrad(0, sum_step(0, 11, 12))
    share_step(0, 0)
    sum_step(1, 9, 11)
    send_weights()
    place(rep, 0)
    share_step(0, 1)
    adagrad(1, sum_step(1, 11, 12))
    share_step(1, 0)
    share_weights()
    place(rep, 1)
    place_step(0, ((1, 0), (1, 6), (2, 0), (2, 6)))
    share_step(0, 2)
    share_step(1, 1)
    place_step(0, ((3, 0), (3, 6), (4, 0), (4, 6)))
    place_step(1, ((1, 0), (1, 6), (2, 0), (2, 6)))
    share_step(1, 2)
    place_step(0, ((5, 0), (5, 6), (6, 0)))
    place_step(1, ((3, 0), (3, 6), (4, 0), (4, 6)))
    wait_bytes(joined.at[pl.ds(0, row - 1)], wj_sem.at[1])
    for spot in range(row):
        for r in range(nr):
            at = r * PIECE + spot * (PIECE // row)
            whole[at : at + PIECE // row, :] = joined[spot, r]
    flat = whole[...]
    out_hidden[...] = flat[:, 0:HID]
    second = flat[:, LANES : 2 * LANES]
    lane_e = iota((E, LANES), 1)
    query_grad = jnp.where(lane_e < room, pltpu.roll(second[0:E], room, 1), pltpu.roll(second[E : 2 * E], LANES - spare + room, 1))
    out_query[...] = query_grad[:, 0:E]
    tail = second[2 * E : 2 * E + 8]
    lane_1 = iota((1, LANES), 1)

    def turn(row, by):
        return pltpu.roll(tail, by, 1)[row : row + 1]

    row_a = jnp.where(lane_1 < room, turn(0, room), jnp.where(lane_1 < 2 * room, turn(1, 2 * room), turn(2, 2 * room - spare)))
    row_b = jnp.where(lane_1 < room, turn(3, room), turn(4, 2 * room))
    out_logit[:, 0:LANES] = row_a
    out_logit[:, LANES:HID] = row_b[:, 0 : HID - LANES]

    place_step(1, ((5, 0), (5, 6), (6, 0)))

    for ref, sem in drains:
        wait_bytes(ref, sem)


def finish(count_of, *refs):
    sources, results, held = (refs[i * count_of : (i + 1) * count_of] for i in range(3))
    sem = refs[-1]
    inward = [pltpu.make_async_copy(sources[i], held[i], sem.at[0, i]) for i in range(count_of)]
    outward = [pltpu.make_async_copy(held[i], results[i], sem.at[1, i]) for i in range(count_of)]
    for copy in inward:
        copy.start()
    for copy_in, copy_out in zip(inward, outward):
        copy_in.wait()
        copy_out.start()
    for copy in outward:
        copy.wait()


def local(
    nt, nr, item_rows, row_accum, w_query, w_hidden, w_logit, wanted_rows, behaviour_slots,
    target_slots, seq_lengths, clicks, fake_flags,
):
    rows = item_rows.shape[0]
    capacity = wanted_rows.shape[2]
    pairs = capacity // 2
    columns = nt * pairs
    seq = behaviour_slots.shape[1]
    per_rep = pairs // nr
    vmem = pl.BlockSpec(memory_space=pltpu.VMEM)
    hbm = pl.BlockSpec(memory_space=pltpu.HBM)
    dma = pltpu.SemaphoreType.DMA
    wide = 2 * LANES
    row = CORES * CHIPS_X
    scratch = [
        pltpu.VMEM((E, rows), F32),
        pltpu.VMEM((rows // LANES, 1, LANES), F32),
        pltpu.VMEM((E, E), F32),
        pltpu.VMEM((3 * E, HID), F32),
        pltpu.VMEM((1, HID), F32),
        pltpu.VMEM((capacity, nt), jnp.int32),
        pltpu.VMEM((USERS, seq), jnp.int32),
        pltpu.SMEM((USERS,), jnp.int32),
        pltpu.SMEM((USERS,), jnp.int32),
        pltpu.SMEM((USERS,), jnp.int32),
        pltpu.SMEM((USERS,), jnp.int32),
        pltpu.VMEM((3 * LANES, rows), BF16),
        pltpu.VMEM((nt, 1, LANES), jnp.int32),
        pltpu.VMEM((nt, 1, LANES), jnp.int32),
        pltpu.VMEM((pairs, LANES, nt), BF16),
        pltpu.VMEM((columns, LANES), F32),
        pltpu.VMEM((columns, LANES), F32),
        pltpu.VMEM((LANES, columns), F32),
        pltpu.VMEM((2 * USERS, columns), F32),
        pltpu.VMEM((2 * USERS, columns), F32),
        pltpu.VMEM((USERS, 1, seq), jnp.int32),
        pltpu.VMEM((USERS, 1, seq), jnp.int32),
        pltpu.VMEM((2 * USERS, columns), F32),
        pltpu.VMEM((2 * USERS, columns), F32),
        pltpu.VMEM((3 * USERS, E, LANES), F32),
        pltpu.VMEM((columns, LANES), F32),
        pltpu.VMEM((nt * early_rows(pairs), LANES), F32),
        pltpu.VMEM((nt * (pairs - early_rows(pairs)), LANES), F32),
        pltpu.VMEM((LANES, 1, LANES), jnp.int32),
        pltpu.VMEM((USERS, 2 * columns // LANES, LANES), F32),
        pltpu.VMEM((nr - 1, per_rep, E, LANES), F32),
        pltpu.VMEM((nr - 1, per_rep, E, LANES), F32),
        pltpu.VMEM((nr * PIECE, wide), F32),
        pltpu.VMEM((nr - 1, PIECE, wide), F32),
        pltpu.VMEM((CORES, PIECE, wide), F32),
        pltpu.VMEM((CHIPS_X, PIECE, wide), F32),
        pltpu.VMEM((nt // (CORES * CHIPS_X), PIECE, wide), F32),
        pltpu.VMEM((row, PIECE // row, wide), F32),
        pltpu.VMEM((nr, PIECE // row, wide), F32),
        pltpu.VMEM((row, nr, PIECE // row, wide), F32),
        pltpu.VMEM((nr * PIECE, wide), F32),
        pltpu.VMEM((nr, per_rep, E + 8, LANES), F32),
        dma((11,)), dma((2,)), dma((2,)), dma((4,)), dma((2,)), dma((2,)), dma((2,)), dma((2,)), dma((2,)), dma((2,)),
        dma((nr - 1, per_rep)), dma((nr - 1, per_rep)), dma((nr - 1, 2)), dma((nr - 1, 2)),
    ]
    results = pl.pallas_call(
        functools.partial(kernel, nt, nr, capacity),
        out_shape=(
            jax.ShapeDtypeStruct((E, rows), F32),
            jax.ShapeDtypeStruct((rows // LANES, 1, LANES), F32),
            jax.ShapeDtypeStruct((E, E), F32),
            jax.ShapeDtypeStruct((3 * E, HID), F32),
            jax.ShapeDtypeStruct((1, HID), F32),
        ),
        in_specs=[hbm] * 11,
        out_specs=[vmem] * 5,
        scratch_shapes=scratch,
        compiler_params=pltpu.CompilerParams(
            collective_id=0, has_side_effects=True, vmem_limit_bytes=VMEM
        ),
    )(
        item_rows.T,
        row_accum.reshape(rows // LANES, 1, LANES),
        w_query,
        w_hidden,
        w_logit.reshape(1, HID),
        wanted_rows[0].T,
        behaviour_slots,
        target_slots,
        seq_lengths,
        clicks,
        fake_flags,
    )
    new_rows, new_accum, grad_query, grad_hidden, grad_logit = pl.pallas_call(
        functools.partial(finish, 5),
        out_shape=[jax.ShapeDtypeStruct(result.shape, result.dtype) for result in results],
        in_specs=[hbm] * 5,
        out_specs=[hbm] * 5,
        scratch_shapes=[pltpu.VMEM(result.shape, result.dtype) for result in results] + [dma((2, 5))],
        compiler_params=pltpu.CompilerParams(vmem_limit_bytes=VMEM),
    )(*results)
    return (new_rows.T, new_accum.reshape(rows), grad_query, grad_hidden, grad_logit.reshape(HID))


def solution(mesh):
    in_specs = (
        P("table", None),
        P("table"),
        P(),
        P(),
        P(),
        P(("table", "rep"), None, None),
        P(("table", "rep"), None),
        P(("table", "rep")),
        P(("table", "rep")),
        P(("table", "rep")),
        P(("table", "rep")),
    )
    out_specs = (P("table", None), P("table"), P(), P(), P())
    return jax.shard_map(
        functools.partial(local, mesh.shape["table"], mesh.shape["rep"]),
        mesh=mesh, in_specs=in_specs, out_specs=out_specs, check_vma=False,
    )
```

```python
import functools

import jax
import jax.numpy as jnp
from jax import lax
from jax.experimental import pallas as pl
from jax.experimental.pallas import tpu as pltpu
from jax.sharding import PartitionSpec as P

FAKE_WEIGHT = 0.3
LEARN_RATE = 0.1
MESH = pl.DeviceIdType.MESH
CORES, CHIPS_X = 2, 4
LANES = 128
E = 64
HID = 200
USERS = 8
PIECE = 16
VMEM = 65000000
F32, BF16 = jnp.float32, jnp.bfloat16


def iota(shape, dim):
    return lax.broadcasted_iota(jnp.int32, shape, dim)


def exact_dot(a, b, contract=((1,), (0,))):
    return lax.dot_general(
        a, b, (contract, ((), ())), precision=lax.Precision.HIGHEST, preferred_element_type=F32
    )


def bf16_dot(a, b, contract=((1,), (0,))):
    return lax.dot_general(a, b, (contract, ((), ())), preferred_element_type=F32)


def split3(x):
    high = x.astype(BF16)
    rest = x - high.astype(F32)
    middle = rest.astype(BF16)
    return high, middle, (rest - middle.astype(F32)).astype(BF16)


def column(ref):
    at = iota((USERS, 1), 0)
    out = jnp.zeros((USERS, 1), jnp.int32)
    for user in range(USERS):
        out = jnp.where(at == user, ref[user], out)
    return out


def place_of(slots, capacity):
    owner = lax.shift_right_logical(slots * 87382, 22)
    entry = slots - owner * capacity
    k = lax.shift_right_logical(entry, 1) & 1
    return owner * (capacity // 2) + k * (capacity // 4) + lax.shift_right_logical(entry, 2), entry & 1


def early_rows(pairs):
    return -(-(pairs // 2) // 8) * 8


def sigmoid(x):
    return 1.0 / (1.0 + jnp.exp(-x))


def kernel(
    nt, nr, capacity,
    items_hbm, accum_hbm, w_query_hbm, w_hidden_hbm, w_logit_hbm, want_hbm, slots_hbm,
    targets_hbm, lengths_hbm, clicks_hbm, flags_hbm,
    out_rows, out_accum, out_query, out_hidden, out_logit,
    items, accum, w_query, w_hidden, w_logit, want, slots, targets, lengths, clicks, flags,
    parts, asked_out, asked, onehot, looked, fetched, keys, count, aimed, code_hi, code_lo,
    weight, dscore, cast, slot_grad, homed_a, homed_b, index_t, named, sums, got,
    weights, weights_z, weights_c, weights_x, weights_y, cuts, spread_out, joined, whole, accums, share,
    in_sem, ask_sem, row_sem, grad_sem, wz_sem, wc_sem, wx_sem, wy_sem, ws_sem, wj_sem, rs_send, rs_recv, ag_send, ag_recv,
):
    me, rep = lax.axis_index("table"), lax.axis_index("rep")
    pairs = capacity // 2
    per_rep = pairs // nr
    columns = nt * pairs
    rows = items_hbm.shape[1]

    def at_rep(distance):
        return lax.rem(rep + nr + distance, nr)

    def block(i):
        return pl.ds(pl.multiple_of(i * pairs, 8), pairs)

    def send(src, dst, sems, to):
        pltpu.make_async_remote_copy(
            src_ref=src, dst_ref=dst, send_sem=sems[0], recv_sem=sems[1], device_id=to, device_id_type=MESH
        ).start()

    def wait_bytes(ref, sem):
        pltpu.make_async_copy(ref, ref, sem).wait()

    drains = []
    brought = [
        pltpu.make_async_copy(src, dst, in_sem.at[i])
        for i, (src, dst) in enumerate([
            (want_hbm, want), (items_hbm, items), (slots_hbm, slots), (lengths_hbm, lengths), (targets_hbm, targets),
            (clicks_hbm, clicks), (flags_hbm, flags), (accum_hbm, accum), (w_query_hbm, w_query),
            (w_hidden_hbm, w_hidden), (w_logit_hbm, w_logit),
        ])
    ]
    brought[0].start()
    core = lax.rem(me, CORES)
    chip_x = lax.rem(lax.div(me, CORES), CHIPS_X)
    chip_y = lax.div(me, CORES * CHIPS_X)
    row = CORES * CHIPS_X
    chips_y = nt // row

    def device(y, x, c):
        return (lax.rem(y, chips_y) * CHIPS_X + lax.rem(x, CHIPS_X)) * CORES + lax.rem(c, CORES)

    def partner(j):
        m = lax.rem(j, chips_y)
        n = lax.rem(lax.div(j, chips_y) + 1, row)
        down, step = lax.rem(m, 2), lax.div(m, 2)
        dy = (chips_y // 2 - step) * (1 - down) + lax.rem(chips_y // 2 + 1 + step, chips_y) * down
        return device(chip_y + dy, chip_x + lax.div(n, CORES), core + lax.rem(n, CORES))

    barrier = pltpu.get_barrier_semaphore()

    @pl.loop(1, nt)
    def _(i):
        pl.semaphore_signal(barrier, inc=1, device_id={"table": lax.rem(me + i, nt)}, device_id_type=MESH)

    @pl.loop(1, nr)
    def _(i):
        pl.semaphore_signal(barrier, inc=1, device_id={"rep": lax.rem(rep + i, nr)}, device_id_type=MESH)

    for copy in brought[1:]:
        copy.start()
    brought[0].wait()
    wanted = jnp.concatenate([want[...], jnp.zeros((LANES - capacity, nt), jnp.int32)], axis=0)
    asked_out[...] = wanted.T.reshape(nt, 1, LANES)
    pl.semaphore_wait(barrier, nt - 1 + nr - 1)

    pltpu.make_async_copy(asked_out.at[me], asked.at[me], ask_sem.at[1]).start()

    @pl.loop(1, nt)
    def _(i):
        to = lax.rem(me + i, nt)
        send(asked_out.at[to], asked.at[me], (ask_sem.at[0], ask_sem.at[1]), {"table": to})

    drains.append((asked.at[pl.ds(0, nt - 1)], ask_sem.at[0]))
    for copy in brought[1:]:
        copy.wait()
    low_half = iota((E, LANES), 1) < E
    wide_low = (iota((E, rows), 1) & (LANES - 1)) < E
    for p, part in enumerate(split3(items[...])):
        part = part.astype(F32)
        parts[p * LANES : p * LANES + E, :] = jnp.where(wide_low, part, 0.0).astype(BF16)
        parts[p * LANES + E : (p + 1) * LANES, :] = jnp.where(wide_low, 0.0, part).astype(BF16)

    wait_bytes(asked, ask_sem.at[1])

    asked_t = jnp.concatenate([asked[...].reshape(nt, LANES), jnp.zeros((LANES - nt, LANES), jnp.int32)], axis=0).T
    first = iota((LANES, nt), 0)
    index_t[...] = asked_t.reshape(LANES, 1, LANES)

    @pl.loop(0, pairs, unroll=8)
    def _(p):
        k = per_rep * p - (per_rep * nr - 1) * lax.div(p, nr)
        at = first + k * LANES
        hot = (at == index_t[2 * k][:, 0:nt]) | (at == index_t[2 * k + 1][:, 0:nt])
        hot = hot.astype(F32).astype(BF16)
        onehot[p] = hot
        found = bf16_dot(parts[:, pl.ds(pl.multiple_of(k * LANES, LANES), LANES)], hot)
        found = found[0:LANES] + found[LANES : 2 * LANES] + found[2 * LANES : 3 * LANES]
        looked[pl.ds(p, nt, stride=pairs), :] = found.T

    groups = 4
    members, group_chunks = nt // groups, columns // LANES // groups
    my_group = lax.div(me, members)

    def send_rows(ahead, i):
        to = lax.rem(my_group + ahead, groups) * members + lax.rem(me + i, members)
        send(looked.at[block(to)], fetched.at[block(me)], (row_sem.at[4], row_sem.at[ahead]), {"table": to})

    pltpu.make_async_copy(looked.at[block(me)], fetched.at[block(me)], row_sem.at[0]).start()

    @pl.loop(0, members)
    def _(i):
        send_rows(2, i)

    @pl.loop(0, members)
    def _(i):
        send_rows(1, i)
        send_rows(3, i)

    @pl.loop(1, members)
    def _(i):
        send_rows(0, i)

    drains.append((looked.at[pl.ds(0, (nt - 1) * pairs)], row_sem.at[4]))
    seq = slots.shape[1]
    place, half = place_of(slots[...], capacity)
    chunks = columns // LANES
    valid = iota((USERS, seq), 1) < column(lengths)
    code_hi[...] = jnp.where(valid, half * chunks + lax.shift_right_logical(place, 7), -1).reshape(USERS, 1, seq)
    code_lo[...] = (place & (LANES - 1)).reshape(USERS, 1, seq)

    @pl.loop(0, USERS)
    def _(user):
        hi = (iota((2 * chunks, seq), 0) == code_hi[user]).astype(F32).astype(BF16)
        lo = (iota((LANES, seq), 0) == code_lo[user]).astype(F32).astype(BF16)
        named[user] = bf16_dot(hi, lo, ((1,), (1,)))

    for h in range(2):
        for c in range(chunks):
            count[h * USERS : (h + 1) * USERS, c * LANES : (c + 1) * LANES] = named[:, h * chunks + c, :]

    target_place, target_half = place_of(column(targets), capacity)
    lane = iota((USERS, columns), 1)
    hit = lane == target_place
    for h in range(2):
        aimed[h * USERS : (h + 1) * USERS, :] = (hit & (target_half == h)).astype(F32)
    weights[:, LANES : 2 * LANES] = jnp.zeros((3 * E, LANES), F32)
    accums[...] = jnp.zeros_like(accums)

    found = jnp.zeros((2 * USERS, LANES), F32)
    for ahead in (2, 1, 3, 0):
        span = group_chunks * LANES
        at = pl.ds(pl.multiple_of(lax.rem(my_group + groups - ahead, groups) * span, LANES), span)
        wait_bytes(fetched.at[at], row_sem.at[ahead])
        picks = aimed[:, at].astype(BF16)
        for p, part in enumerate(split3(fetched[at, :])):
            keys[p, at, :] = part
            found = found + bf16_dot(picks, part)

    def stacked_dot(x, contract):
        high, middle, low = split3(x)
        n = x.shape[0]
        first = bf16_dot(jnp.concatenate([high, middle, low], axis=0), keys[0], contract)
        second = bf16_dot(jnp.concatenate([high, middle], axis=0), keys[1], contract)
        third = bf16_dot(high, keys[2], contract)
        return first[0:n] + ((first[n : 2 * n] + second[0:n]) + (first[2 * n : 3 * n] + second[n : 2 * n] + third))

    along, across = ((1,), (0,)), ((1,), (1,))

    def fold(x):
        return x[0:USERS, 0:E] + x[USERS : 2 * USERS, E : 2 * E]

    def spread(x):
        zero = jnp.zeros_like(x)
        return jnp.concatenate(
            [jnp.concatenate([x, zero], axis=1), jnp.concatenate([zero, x], axis=1)], axis=0
        )

    def both(x):
        return jnp.concatenate([x, x], axis=0)

    target = fold(found)
    query = exact_dot(target, w_query[...]) * E ** (-0.5)
    scores = stacked_dot(spread(query), across)
    times = count[...]
    present = times > 0.0
    scores = jnp.where(present, scores, -1e30)
    largest = jnp.max(scores, axis=1, keepdims=True)
    largest = both(jnp.maximum(largest[0:USERS], largest[USERS : 2 * USERS]))
    raised = jnp.where(present, jnp.exp(scores - largest), 0.0)
    total = jnp.sum(raised * times, axis=1, keepdims=True)
    total = both(total[0:USERS] + total[USERS : 2 * USERS])
    attention = raised / total
    weight[...] = attention
    pooled = fold(stacked_dot(attention * times, along))
    features = jnp.concatenate([pooled, target, pooled * target], axis=1)
    before = exact_dot(features, w_hidden[...])
    gate = sigmoid(before)
    hidden = before * gate
    logit = jnp.sum(hidden * w_logit[...], axis=1, keepdims=True)
    click = column(clicks)
    scale = jnp.where(click == 1, 1.0, jnp.where(column(flags) == 1, FAKE_WEIGHT, 1.0)).astype(F32)
    d_logit = scale * (sigmoid(logit) - click.astype(F32))
    d_before = d_logit * w_logit[...] * (gate + hidden * (1.0 - gate))
    weights[:, 0:HID] = exact_dot(features.T, d_before)
    d_w_logit = jnp.sum(hidden * d_logit, axis=0, keepdims=True)
    d_features = exact_dot(d_before, w_hidden[...], ((1,), (1,)))
    d_cross = d_features[:, 2 * E : 3 * E]
    d_pooled = d_features[:, 0:E] + d_cross * target
    d_target = d_features[:, E : 2 * E] + d_cross * pooled
    pull = stacked_dot(spread(d_pooled), across)
    shift = jnp.sum(pooled * d_pooled, axis=1, keepdims=True)
    d_scores = attention * (pull - both(shift))
    dscore[...] = d_scores
    d_query = fold(stacked_dot(d_scores * times, along)) * E ** (-0.5)
    d_target = d_target + exact_dot(d_query, w_query[...], ((1,), (1,)))
    d_w_query = exact_dot(target.T, d_query)
    spare = HID - LANES
    room = LANES - spare
    low = jnp.concatenate([d_w_query, jnp.zeros((E, LANES - E), F32)], axis=1)
    row_a = d_w_logit[:, 0:LANES]
    row_b = jnp.concatenate([d_w_logit[:, LANES:HID], jnp.zeros((1, room), F32)], axis=1)
    logit_rows = [
        pltpu.roll(row_a, spare, 1), pltpu.roll(row_a, spare - room, 1), pltpu.roll(row_a, spare + LANES - 2 * room, 1),
        pltpu.roll(row_b, spare, 1), pltpu.roll(row_b, spare - room, 1), jnp.zeros((E - 5, LANES), F32),
    ]
    extra = [pltpu.roll(low, spare, 1), pltpu.roll(low, spare - room, 1)] + logit_rows
    second = weights[:, LANES : 2 * LANES]
    free = iota((3 * E, LANES), 1) >= spare
    weights[:, LANES : 2 * LANES] = jnp.where(free, jnp.concatenate(extra, axis=0), second)

    @pl.loop(1, nr)
    def _(i):
        to = lax.rem(rep + i, nr)
        piece = weights.at[pl.ds(pl.multiple_of(to * PIECE, 8), PIECE)]
        send(piece, weights_z.at[i - 1], (wz_sem.at[0], wz_sem.at[1]), {"rep": to})

    drains.append((weights_z, wz_sem.at[0]))
    vectors = jnp.concatenate([d_pooled, query, d_target], axis=0)
    vectors = jnp.concatenate([vectors, jnp.zeros((3 * USERS, LANES - E), F32)], axis=1)
    vectors = jnp.concatenate([vectors, jnp.zeros((LANES - 3 * USERS, LANES), F32)], axis=0).T
    for i in range(3 * USERS):
        cast[i] = jnp.broadcast_to(vectors[0:E, i : i + 1], (E, LANES))

    def slot_grads(c):
        at = pl.ds(pl.multiple_of(c * LANES, LANES), LANES)
        w_c, s_c, n_c, a_c = weight[:, at], dscore[:, at], count[:, at], aimed[:, at]
        halves = []
        for h in range(2):
            acc = jnp.zeros((E, LANES), F32)
            for u in range(USERS):
                row = slice(h * USERS + u, h * USERS + u + 1)
                key_grad = w_c[row] * cast[u] + s_c[row] * cast[USERS + u]
                key_grad = key_grad.astype(BF16).astype(F32)
                acc = acc + n_c[row] * key_grad + a_c[row] * cast[2 * USERS + u]
            halves.append(acc)
        slot_grad[at, :] = jnp.concatenate(halves, axis=0).T

    def send_grads(to, landing, first_row, count_of, sems):
        src = slot_grad.at[pl.ds(pl.multiple_of(to * pairs + first_row, 8), count_of)]
        dst = landing.at[pl.ds(pl.multiple_of(me * count_of, 8), count_of)]

        @pl.when(to != me)
        def _():
            send(src, dst, sems, {"table": to})

        @pl.when(to == me)
        def _():
            pltpu.make_async_copy(src, dst, sems[1]).start()

    early = early_rows(pairs)
    late = pairs - early
    for g in (2, 1, 3, 0):
        group = lax.rem(my_group + g, groups)

        for i in range(group_chunks):
            slot_grads(group * group_chunks + i)
            low, high = i * LANES // pairs, (i + 1) * LANES // pairs

            @pl.loop(0, high - low)
            def _(m):
                to = group * members + low + lax.rem(me + m, high - low)
                send_grads(to, homed_a, 0, early, (grad_sem.at[0], grad_sem.at[1]))

    @pl.loop(0, nt)
    def _(j):
        send_grads(partner(j), homed_b, early, late, (grad_sem.at[2], grad_sem.at[3]))

    drains.append((homed_a.at[pl.ds(0, (nt - 1) * early)], grad_sem.at[0]))
    drains.append((homed_b.at[pl.ds(0, (nt - 1) * late)], grad_sem.at[2]))
    wait_bytes(weights_z, wz_sem.at[1])
    piece = weights[pl.ds(pl.multiple_of(rep * PIECE, 8), PIECE), :]
    for i in range(nr - 1):
        piece = piece + weights_z[i]
    def add_up(ref, count_of):
        out = ref[0]
        for i in range(1, count_of):
            out = out + ref[i]
        return out

    def send_cores():
        weights_c[core] = piece
        send(weights_c.at[core], weights_c.at[core], (wc_sem.at[0], wc_sem.at[1]), {"table": me + 1 - 2 * core})
        drains.append((weights_c.at[0], wc_sem.at[0]))

    def send_x():
        drains.append((weights_x.at[pl.ds(0, CHIPS_X - 1)], wx_sem.at[0]))
        wait_bytes(weights_c.at[0], wc_sem.at[1])
        weights_x[chip_x] = add_up(weights_c, CORES)

        @pl.loop(1, CHIPS_X)
        def _(i):
            to = lax.rem(chip_x + i, CHIPS_X)
            send(weights_x.at[chip_x], weights_x.at[chip_x], (wx_sem.at[0], wx_sem.at[1]),
                 {"table": (chip_y * CHIPS_X + to) * CORES + core})

    def send_y():
        drains.append((weights_y.at[pl.ds(0, chips_y - 1)], wy_sem.at[0]))
        wait_bytes(weights_x.at[pl.ds(0, CHIPS_X - 1)], wx_sem.at[1])
        weights_y[chip_y] = add_up(weights_x, CHIPS_X)

        @pl.loop(1, chips_y)
        def _(i):
            to = lax.rem(chip_y + i, chips_y)
            send(weights_y.at[chip_y], weights_y.at[chip_y], (wy_sem.at[0], wy_sem.at[1]),
                 {"table": (to * CHIPS_X + chip_x) * CORES + core})

    def send_weights():
        wait_bytes(weights_y.at[pl.ds(0, chips_y - 1)], wy_sem.at[1])
        total = add_up(weights_y, chips_y)
        for spot in range(row):
            cuts[spot] = total[spot * PIECE // row : (spot + 1) * PIECE // row]
        spread_out[rep] = cuts[lax.rem(me, row)]

        @pl.loop(1, nr)
        def _(i):
            to = lax.rem(rep + i, nr)
            send(spread_out.at[rep], spread_out.at[rep], (ws_sem.at[0], ws_sem.at[1]), {"rep": to})

        drains.append((spread_out.at[pl.ds(0, nr - 1)], ws_sem.at[0]))

    def share_weights():
        wait_bytes(spread_out.at[pl.ds(0, nr - 1)], ws_sem.at[1])
        spot = lax.rem(me, row)
        joined[spot] = spread_out[...]

        @pl.loop(1, row)
        def _(i):
            to = chip_y * row + lax.rem(spot + i, row)
            send(joined.at[spot], joined.at[spot], (wj_sem.at[0], wj_sem.at[1]), {"table": to})

        drains.append((joined.at[pl.ds(0, row - 1)], wj_sem.at[0]))

    def own(dest, k):
        at = k * nr + dest
        if k == 0:
            rows_of = homed_a[pl.ds(at, nt, stride=early), :]
        else:
            ahead = at < early
            in_a = homed_a[pl.ds(jnp.minimum(at, early - 1), nt, stride=early), :]
            in_b = homed_b[pl.ds(jnp.maximum(at - early, 0), nt, stride=late), :]
            rows_of = jnp.where(ahead, in_a, in_b)
        here = bf16_dot(onehot[at], jnp.concatenate(split3(rows_of), axis=1))
        here = here[:, 0:LANES] + here[:, LANES : 2 * LANES] + here[:, 2 * LANES : 3 * LANES]
        return jnp.where(low_half, here[0:E], here[E : 2 * E])

    strides = (2, 2)
    sign = (1, -1)
    reaches = ((nr // 2, 1), (nr - 1 - nr // 2, -1))

    def plan_of(stride):
        stages = {}
        slot = {}
        for reach, way in reaches:
            for distance in range(reach, 0, -1):
                level = distance // stride if distance % stride == 0 and distance < reach else None
                slot[distance * way] = len(slot)
                terms = () if level is None else tuple(
                    slot[way * d] for d in range(distance + 1, min(distance + stride, reach) + 1)
                )
                hop = (distance - 1) % stride + 1
                stages.setdefault(level, []).append((slot[distance * way], distance * way, hop * way, terms))
        top = max(level for level in stages if level is not None)
        leaves = sorted(stages[None], key=lambda item: -abs(item[1]))
        last = tuple(slot[way * d] for reach, way in reaches for d in range(1, stride + 1))
        return [leaves] + [stages[level] for level in range(top, 0, -1)] + [[(None, 0, 0, last)]]

    plans = [plan_of(stride) for stride in strides]

    def sum_stage(k, stage):
        items_of = plans[k][stage]
        for start in range(0, len(items_of), 3):
            batch = items_of[start : start + 3]
            values = [own(at_rep(sign[k] * far), k) for _, far, _, _ in batch]
            for value, (slot, _, hop, terms) in zip(values, batch):
                for term in terms:
                    wait_bytes(got.at[term, k], rs_recv.at[term, k])
                    value = value + got[term, k]
                if slot is None:
                    return value
                sums[slot, k] = value
                send(sums.at[slot, k], got.at[slot, k], (rs_send.at[slot, k], rs_recv.at[slot, k]), {"rep": at_rep(sign[k] * hop)})
                drains.append((sums.at[slot, k], rs_send.at[slot, k]))

    def adagrad(k, value):
        turned = jnp.concatenate([value, jnp.zeros_like(value)], axis=0).T
        grads = jnp.where(low_half, turned[0:E], pltpu.roll(turned[E : 2 * E], E, 1))
        at = rep * per_rep + k
        new_accum = accum[at] + jnp.sum(grads * grads, axis=0, keepdims=True) * (1.0 / E)
        old = items[:, pl.ds(pl.multiple_of(at * LANES, LANES), LANES)]
        share[rep, k, 0:E, :] = old - LEARN_RATE * grads / jnp.sqrt(new_accum)
        accums[k : k + 1, :] = new_accum
        if k == per_rep - 1:
            share[rep, k, E : E + 8, :] = accums[...]

    def place(r, k):
        at = r * per_rep + k
        out_rows[:, pl.ds(pl.multiple_of(at * LANES, LANES), LANES)] = share[r, k, 0:E, :]
        if k == per_rep - 1:
            for i in range(per_rep):
                out_accum[r * per_rep + i] = share[r, k, E + i : E + i + 1, :]

    def block_of(r, k):
        return share.at[r, k, pl.ds(0, E + 8 * (k == per_rep - 1))]

    def share_stage(k, stage):
        stride = strides[k]
        for reach, way in reaches:
            side = 0 if way == 1 else nr // 2
            part = block_of(at_rep(-sign[k] * way * stride * stage), k)
            if stage and stride * stage < reach:
                wait_bytes(part, ag_recv.at[side + stride * stage - 1, k])
            for hop in range(stride, 0, -1):
                distance = stride * stage + hop
                if distance <= reach:
                    at = side + distance - 1
                    send(part, part, (ag_send.at[at, k], ag_recv.at[at, k]), {"rep": at_rep(sign[k] * way * hop)})
                    drains.append((part, ag_send.at[at, k]))

    def place_stage(k, stage):
        stride = strides[k]
        for hop in range(1, stride + 1):
            for reach, way in reaches:
                side = 0 if way == 1 else nr // 2
                distance = stride * stage + hop
                if distance <= reach:
                    source = at_rep(-sign[k] * way * distance)
                    if distance % stride or distance == reach:
                        wait_bytes(block_of(source, k), ag_recv.at[side + distance - 1, k])
                    place(source, k)

    send_cores()
    wait_bytes(homed_a, grad_sem.at[1])
    sum_stage(0, 0)
    sum_stage(0, 1)
    wait_bytes(homed_b, grad_sem.at[3])
    sum_stage(1, 0)
    send_x()
    sum_stage(0, 2)
    sum_stage(1, 1)
    send_y()
    adagrad(0, sum_stage(0, 3))
    share_stage(0, 0)
    sum_stage(1, 2)
    send_weights()
    place(rep, 0)
    share_stage(0, 1)
    adagrad(1, sum_stage(1, 3))
    share_stage(1, 0)
    share_weights()
    place(rep, 1)
    share_stage(0, 2)
    place_stage(0, 0)
    share_stage(1, 1)
    place_stage(0, 1)
    place_stage(1, 0)
    share_stage(1, 2)
    place_stage(0, 2)
    place_stage(1, 1)
    wait_bytes(joined.at[pl.ds(0, row - 1)], wj_sem.at[1])
    for spot in range(row):
        for r in range(nr):
            at = r * PIECE + spot * (PIECE // row)
            whole[at : at + PIECE // row, :] = joined[spot, r]
    flat = whole[...]
    out_hidden[...] = flat[:, 0:HID]
    second = flat[:, LANES : 2 * LANES]
    lane_e = iota((E, LANES), 1)
    query_grad = jnp.where(lane_e < room, pltpu.roll(second[0:E], room, 1), pltpu.roll(second[E : 2 * E], LANES - spare + room, 1))
    out_query[...] = query_grad[:, 0:E]
    tail = second[2 * E : 2 * E + 8]
    lane_1 = iota((1, LANES), 1)

    def turn(row, by):
        return pltpu.roll(tail, by, 1)[row : row + 1]

    row_a = jnp.where(lane_1 < room, turn(0, room), jnp.where(lane_1 < 2 * room, turn(1, 2 * room), turn(2, 2 * room - spare)))
    row_b = jnp.where(lane_1 < room, turn(3, room), turn(4, 2 * room))
    out_logit[:, 0:LANES] = row_a
    out_logit[:, LANES:HID] = row_b[:, 0 : HID - LANES]

    place_stage(1, 2)

    for ref, sem in drains:
        wait_bytes(ref, sem)


def finish(count_of, *refs):
    sem = refs[-1]
    copies = [pltpu.make_async_copy(refs[i], refs[count_of + i], sem.at[i]) for i in range(count_of)]
    for copy in copies:
        copy.start()
    for copy in copies:
        copy.wait()


def local(
    nt, nr, item_rows, row_accum, w_query, w_hidden, w_logit, wanted_rows, behaviour_slots,
    target_slots, seq_lengths, clicks, fake_flags,
):
    rows = item_rows.shape[0]
    capacity = wanted_rows.shape[2]
    pairs = capacity // 2
    columns = nt * pairs
    seq = behaviour_slots.shape[1]
    per_rep = pairs // nr
    vmem = pl.BlockSpec(memory_space=pltpu.VMEM)

    def in_hbm(x):
        return pltpu.with_memory_space_constraint(x, pltpu.HBM)

    hbm = pl.BlockSpec(memory_space=pltpu.HBM)
    dma = pltpu.SemaphoreType.DMA
    wide = 2 * LANES
    row = CORES * CHIPS_X
    scratch = [
        pltpu.VMEM((E, rows), F32),
        pltpu.VMEM((rows // LANES, 1, LANES), F32),
        pltpu.VMEM((E, E), F32),
        pltpu.VMEM((3 * E, HID), F32),
        pltpu.VMEM((1, HID), F32),
        pltpu.VMEM((capacity, nt), jnp.int32),
        pltpu.VMEM((USERS, seq), jnp.int32),
        pltpu.SMEM((USERS,), jnp.int32),
        pltpu.SMEM((USERS,), jnp.int32),
        pltpu.SMEM((USERS,), jnp.int32),
        pltpu.SMEM((USERS,), jnp.int32),
        pltpu.VMEM((3 * LANES, rows), BF16),
        pltpu.VMEM((nt, 1, LANES), jnp.int32),
        pltpu.VMEM((nt, 1, LANES), jnp.int32),
        pltpu.VMEM((pairs, LANES, nt), BF16),
        pltpu.VMEM((columns, LANES), F32),
        pltpu.VMEM((columns, LANES), F32),
        pltpu.VMEM((3, columns, LANES), BF16),
        pltpu.VMEM((2 * USERS, columns), F32),
        pltpu.VMEM((2 * USERS, columns), F32),
        pltpu.VMEM((USERS, 1, seq), jnp.int32),
        pltpu.VMEM((USERS, 1, seq), jnp.int32),
        pltpu.VMEM((2 * USERS, columns), F32),
        pltpu.VMEM((2 * USERS, columns), F32),
        pltpu.VMEM((3 * USERS, E, LANES), F32),
        pltpu.VMEM((columns, LANES), F32),
        pltpu.VMEM((nt * early_rows(pairs), LANES), F32),
        pltpu.VMEM((nt * (pairs - early_rows(pairs)), LANES), F32),
        pltpu.VMEM((LANES, 1, LANES), jnp.int32),
        pltpu.VMEM((USERS, 2 * columns // LANES, LANES), F32),
        pltpu.VMEM((nr - 1, per_rep, E, LANES), F32),
        pltpu.VMEM((nr - 1, per_rep, E, LANES), F32),
        pltpu.VMEM((nr * PIECE, wide), F32),
        pltpu.VMEM((nr - 1, PIECE, wide), F32),
        pltpu.VMEM((CORES, PIECE, wide), F32),
        pltpu.VMEM((CHIPS_X, PIECE, wide), F32),
        pltpu.VMEM((nt // (CORES * CHIPS_X), PIECE, wide), F32),
        pltpu.VMEM((row, PIECE // row, wide), F32),
        pltpu.VMEM((nr, PIECE // row, wide), F32),
        pltpu.VMEM((row, nr, PIECE // row, wide), F32),
        pltpu.VMEM((nr * PIECE, wide), F32),
        pltpu.VMEM((8, LANES), F32),
        pltpu.VMEM((nr, per_rep, E + 8, LANES), F32),
        dma((11,)), dma((2,)), dma((5,)), dma((4,)), dma((2,)), dma((2,)), dma((2,)), dma((2,)), dma((2,)), dma((2,)),
        dma((nr - 1, per_rep)), dma((nr - 1, per_rep)), dma((nr - 1, 2)), dma((nr - 1, 2)),
    ]
    results = pl.pallas_call(
        functools.partial(kernel, nt, nr, capacity),
        out_shape=(
            pltpu.VMEM((E, rows), F32),
            pltpu.VMEM((rows // LANES, 1, LANES), F32),
            pltpu.VMEM((E, E), F32),
            pltpu.VMEM((3 * E, HID), F32),
            pltpu.VMEM((1, HID), F32),
        ),
        in_specs=[hbm] * 11,
        out_specs=[vmem] * 5,
        scratch_shapes=scratch,
        compiler_params=pltpu.CompilerParams(
            collective_id=0, has_side_effects=True, vmem_limit_bytes=VMEM
        ),
    )(
        in_hbm(item_rows.T),
        in_hbm(row_accum.reshape(rows // LANES, 1, LANES)),
        in_hbm(w_query),
        in_hbm(w_hidden),
        in_hbm(w_logit.reshape(1, HID)),
        in_hbm(wanted_rows[0].T),
        in_hbm(behaviour_slots),
        in_hbm(target_slots),
        in_hbm(seq_lengths),
        in_hbm(clicks),
        in_hbm(fake_flags),
    )
    new_rows, new_accum, grad_query, grad_hidden, grad_logit = pl.pallas_call(
        functools.partial(finish, 5),
        out_shape=[jax.ShapeDtypeStruct(result.shape, result.dtype) for result in results],
        in_specs=[vmem] * 5,
        out_specs=[hbm] * 5,
        scratch_shapes=[dma((5,))],
        compiler_params=pltpu.CompilerParams(vmem_limit_bytes=VMEM),
    )(*[pltpu.with_memory_space_constraint(result, pltpu.VMEM) for result in results])
    return (new_rows.T, new_accum.reshape(rows), grad_query, grad_hidden, grad_logit.reshape(HID))


def solution(mesh):
    in_specs = (
        P("table", None),
        P("table"),
        P(),
        P(),
        P(),
        P(("table", "rep"), None, None),
        P(("table", "rep"), None),
        P(("table", "rep")),
        P(("table", "rep")),
        P(("table", "rep")),
        P(("table", "rep")),
    )
    out_specs = (P("table", None), P("table"), P(), P(), P())
    return jax.shard_map(
        functools.partial(local, mesh.shape["table"], mesh.shape["rep"]),
        mesh=mesh, in_specs=in_specs, out_specs=out_specs, check_vma=False,
    )
```

```python
import functools

import jax
import jax.numpy as jnp
from jax import lax
from jax.experimental import pallas as pl
from jax.experimental.pallas import tpu as pltpu
from jax.sharding import PartitionSpec as P

FAKE_WEIGHT = 0.3
LEARN_RATE = 0.1
MESH = pl.DeviceIdType.MESH
CORES, CHIPS_X = 2, 4
LANES = 128
E = 64
HID = 200
USERS = 8
PIECE = 16
VMEM = 65000000
F32, BF16 = jnp.float32, jnp.bfloat16


def iota(shape, dim):
    return lax.broadcasted_iota(jnp.int32, shape, dim)


def exact_dot(a, b, contract=((1,), (0,))):
    return lax.dot_general(
        a, b, (contract, ((), ())), precision=lax.Precision.HIGHEST, preferred_element_type=F32
    )


def bf16_dot(a, b, contract=((1,), (0,))):
    return lax.dot_general(a, b, (contract, ((), ())), preferred_element_type=F32)


def split3(x):
    high = x.astype(BF16)
    rest = x - high.astype(F32)
    middle = rest.astype(BF16)
    return high, middle, (rest - middle.astype(F32)).astype(BF16)


def column(ref):
    at = iota((USERS, 1), 0)
    out = jnp.zeros((USERS, 1), jnp.int32)
    for user in range(USERS):
        out = jnp.where(at == user, ref[user], out)
    return out


def place_of(slots, capacity):
    owner = lax.shift_right_logical(slots * 87382, 22)
    entry = slots - owner * capacity
    k = lax.shift_right_logical(entry, 1) & 1
    return owner * (capacity // 2) + k * (capacity // 4) + lax.shift_right_logical(entry, 2), entry & 1


def early_rows(pairs):
    return -(-(pairs // 2) // 8) * 8


def sigmoid(x):
    return 1.0 / (1.0 + jnp.exp(-x))


def kernel(
    nt, nr, capacity,
    items_hbm, accum_hbm, w_query_hbm, w_hidden_hbm, w_logit_hbm, want_hbm, slots_hbm,
    targets_hbm, lengths_hbm, clicks_hbm, flags_hbm,
    out_rows, out_accum, out_query, out_hidden, out_logit,
    items, accum, w_query, w_hidden, w_logit, want, slots, targets, lengths, clicks, flags,
    parts, asked_out, asked, onehot, looked, fetched, keys, count, aimed, code_hi, code_lo,
    weight, dscore, cast, slot_grad, homed_a, homed_b, index_t, named, sums, got,
    weights, weights_z, weights_c, weights_x, weights_y, cuts, spread_out, joined, whole, accums, share,
    in_sem, ask_sem, row_sem, grad_sem, wz_sem, wc_sem, wx_sem, wy_sem, ws_sem, wj_sem, rs_send, rs_recv, ag_send, ag_recv,
):
    me, rep = lax.axis_index("table"), lax.axis_index("rep")
    pairs = capacity // 2
    per_rep = pairs // nr
    columns = nt * pairs
    rows = items_hbm.shape[1]

    def at_rep(distance):
        return lax.rem(rep + nr + distance, nr)

    def block(i):
        return pl.ds(pl.multiple_of(i * pairs, 8), pairs)

    def send(src, dst, sems, to):
        pltpu.make_async_remote_copy(
            src_ref=src, dst_ref=dst, send_sem=sems[0], recv_sem=sems[1], device_id=to, device_id_type=MESH
        ).start()

    def wait_bytes(ref, sem):
        pltpu.make_async_copy(ref, ref, sem).wait()

    drains = []
    brought = [
        pltpu.make_async_copy(src, dst, in_sem.at[i])
        for i, (src, dst) in enumerate([
            (want_hbm, want), (items_hbm, items), (slots_hbm, slots), (lengths_hbm, lengths), (targets_hbm, targets),
            (clicks_hbm, clicks), (flags_hbm, flags), (accum_hbm, accum), (w_query_hbm, w_query),
            (w_hidden_hbm, w_hidden), (w_logit_hbm, w_logit),
        ])
    ]
    brought[0].start()
    core = lax.rem(me, CORES)
    chip_x = lax.rem(lax.div(me, CORES), CHIPS_X)
    chip_y = lax.div(me, CORES * CHIPS_X)
    row = CORES * CHIPS_X
    chips_y = nt // row

    def device(y, x, c):
        return (lax.rem(y, chips_y) * CHIPS_X + lax.rem(x, CHIPS_X)) * CORES + lax.rem(c, CORES)

    def partner(j):
        m = lax.rem(j, chips_y)
        n = lax.rem(lax.div(j, chips_y) + 1, row)
        down, step = lax.rem(m, 2), lax.div(m, 2)
        dy = (chips_y // 2 - step) * (1 - down) + lax.rem(chips_y // 2 + 1 + step, chips_y) * down
        return device(chip_y + dy, chip_x + lax.div(n, CORES), core + lax.rem(n, CORES))

    barrier = pltpu.get_barrier_semaphore()

    @pl.loop(1, nt)
    def _(i):
        pl.semaphore_signal(barrier, inc=1, device_id={"table": lax.rem(me + i, nt)}, device_id_type=MESH)

    @pl.loop(1, nr)
    def _(i):
        pl.semaphore_signal(barrier, inc=1, device_id={"rep": lax.rem(rep + i, nr)}, device_id_type=MESH)

    for copy in brought[1:]:
        copy.start()
    brought[0].wait()
    wanted = jnp.concatenate([want[...], jnp.zeros((LANES - capacity, nt), jnp.int32)], axis=0)
    asked_out[...] = wanted.T.reshape(nt, 1, LANES)
    pl.semaphore_wait(barrier, nt - 1 + nr - 1)

    pltpu.make_async_copy(asked_out.at[me], asked.at[me], ask_sem.at[1]).start()

    @pl.loop(1, nt)
    def _(i):
        to = lax.rem(me + i, nt)
        send(asked_out.at[to], asked.at[me], (ask_sem.at[0], ask_sem.at[1]), {"table": to})

    drains.append((asked.at[pl.ds(0, nt - 1)], ask_sem.at[0]))
    for copy in brought[1:]:
        copy.wait()
    low_half = iota((E, LANES), 1) < E
    wide_low = (iota((E, rows), 1) & (LANES - 1)) < E
    for p, part in enumerate(split3(items[...])):
        part = part.astype(F32)
        parts[p * LANES : p * LANES + E, :] = jnp.where(wide_low, part, 0.0).astype(BF16)
        parts[p * LANES + E : (p + 1) * LANES, :] = jnp.where(wide_low, 0.0, part).astype(BF16)

    wait_bytes(asked, ask_sem.at[1])

    asked_t = jnp.concatenate([asked[...].reshape(nt, LANES), jnp.zeros((LANES - nt, LANES), jnp.int32)], axis=0).T
    first = iota((LANES, nt), 0)
    index_t[...] = asked_t.reshape(LANES, 1, LANES)

    @pl.loop(0, pairs, unroll=8)
    def _(p):
        k = per_rep * p - (per_rep * nr - 1) * lax.div(p, nr)
        at = first + k * LANES
        hot = (at == index_t[2 * k][:, 0:nt]) | (at == index_t[2 * k + 1][:, 0:nt])
        hot = hot.astype(F32).astype(BF16)
        onehot[p] = hot
        found = bf16_dot(parts[:, pl.ds(pl.multiple_of(k * LANES, LANES), LANES)], hot)
        found = found[0:LANES] + found[LANES : 2 * LANES] + found[2 * LANES : 3 * LANES]
        looked[pl.ds(p, nt, stride=pairs), :] = found.T

    groups = 4
    members, group_chunks = nt // groups, columns // LANES // groups
    my_group = lax.div(me, members)

    def send_rows(ahead, i):
        to = lax.rem(my_group + ahead, groups) * members + lax.rem(me + i, members)
        send(looked.at[block(to)], fetched.at[block(me)], (row_sem.at[4], row_sem.at[ahead]), {"table": to})

    pltpu.make_async_copy(looked.at[block(me)], fetched.at[block(me)], row_sem.at[0]).start()

    @pl.loop(0, members)
    def _(i):
        send_rows(2, i)

    @pl.loop(0, members)
    def _(i):
        send_rows(1, i)
        send_rows(3, i)

    @pl.loop(1, members)
    def _(i):
        send_rows(0, i)

    drains.append((looked.at[pl.ds(0, (nt - 1) * pairs)], row_sem.at[4]))
    seq = slots.shape[1]
    place, half = place_of(slots[...], capacity)
    chunks = columns // LANES
    valid = iota((USERS, seq), 1) < column(lengths)
    code_hi[...] = jnp.where(valid, half * chunks + lax.shift_right_logical(place, 7), -1).reshape(USERS, 1, seq)
    code_lo[...] = (place & (LANES - 1)).reshape(USERS, 1, seq)

    @pl.loop(0, USERS)
    def _(user):
        hi = (iota((2 * chunks, seq), 0) == code_hi[user]).astype(F32).astype(BF16)
        lo = (iota((LANES, seq), 0) == code_lo[user]).astype(F32).astype(BF16)
        named[user] = bf16_dot(hi, lo, ((1,), (1,)))

    for h in range(2):
        for c in range(chunks):
            count[h * USERS : (h + 1) * USERS, c * LANES : (c + 1) * LANES] = named[:, h * chunks + c, :]

    target_place, target_half = place_of(column(targets), capacity)
    lane = iota((USERS, columns), 1)
    hit = lane == target_place
    for h in range(2):
        aimed[h * USERS : (h + 1) * USERS, :] = (hit & (target_half == h)).astype(F32)
    weights[:, LANES : 2 * LANES] = jnp.zeros((3 * E, LANES), F32)
    accums[...] = jnp.zeros_like(accums)

    found = jnp.zeros((2 * USERS, LANES), F32)
    for ahead in (2, 1, 3, 0):
        span = group_chunks * LANES
        at = pl.ds(pl.multiple_of(lax.rem(my_group + groups - ahead, groups) * span, LANES), span)
        wait_bytes(fetched.at[at], row_sem.at[ahead])
        picks = aimed[:, at].astype(BF16)
        for p, part in enumerate(split3(fetched[at, :])):
            keys[p, at, :] = part
            found = found + bf16_dot(picks, part)

    def stacked_dot(x, contract):
        high, middle, low = split3(x)
        n = x.shape[0]
        first = bf16_dot(jnp.concatenate([high, middle, low], axis=0), keys[0], contract)
        second = bf16_dot(jnp.concatenate([high, middle], axis=0), keys[1], contract)
        third = bf16_dot(high, keys[2], contract)
        return first[0:n] + ((first[n : 2 * n] + second[0:n]) + (first[2 * n : 3 * n] + second[n : 2 * n] + third))

    along, across = ((1,), (0,)), ((1,), (1,))

    def fold(x):
        return x[0:USERS, 0:E] + x[USERS : 2 * USERS, E : 2 * E]

    def spread(x):
        zero = jnp.zeros_like(x)
        return jnp.concatenate(
            [jnp.concatenate([x, zero], axis=1), jnp.concatenate([zero, x], axis=1)], axis=0
        )

    def both(x):
        return jnp.concatenate([x, x], axis=0)

    target = fold(found)
    query = exact_dot(target, w_query[...]) * E ** (-0.5)
    scores = stacked_dot(spread(query), across)
    times = count[...]
    present = times > 0.0
    scores = jnp.where(present, scores, -1e30)
    largest = jnp.max(scores, axis=1, keepdims=True)
    largest = both(jnp.maximum(largest[0:USERS], largest[USERS : 2 * USERS]))
    raised = jnp.where(present, jnp.exp(scores - largest), 0.0)
    total = jnp.sum(raised * times, axis=1, keepdims=True)
    total = both(total[0:USERS] + total[USERS : 2 * USERS])
    attention = raised / total
    weight[...] = attention
    pooled = fold(stacked_dot(attention * times, along))
    features = jnp.concatenate([pooled, target, pooled * target], axis=1)
    before = exact_dot(features, w_hidden[...])
    gate = sigmoid(before)
    hidden = before * gate
    logit = jnp.sum(hidden * w_logit[...], axis=1, keepdims=True)
    click = column(clicks)
    scale = jnp.where(click == 1, 1.0, jnp.where(column(flags) == 1, FAKE_WEIGHT, 1.0)).astype(F32)
    d_logit = scale * (sigmoid(logit) - click.astype(F32))
    d_before = d_logit * w_logit[...] * (gate + hidden * (1.0 - gate))
    weights[:, 0:HID] = exact_dot(features.T, d_before)
    d_w_logit = jnp.sum(hidden * d_logit, axis=0, keepdims=True)
    d_features = exact_dot(d_before, w_hidden[...], ((1,), (1,)))
    d_cross = d_features[:, 2 * E : 3 * E]
    d_pooled = d_features[:, 0:E] + d_cross * target
    d_target = d_features[:, E : 2 * E] + d_cross * pooled
    pull = stacked_dot(spread(d_pooled), across)
    shift = jnp.sum(pooled * d_pooled, axis=1, keepdims=True)
    d_scores = attention * (pull - both(shift))
    dscore[...] = d_scores
    d_query = fold(stacked_dot(d_scores * times, along)) * E ** (-0.5)
    d_target = d_target + exact_dot(d_query, w_query[...], ((1,), (1,)))
    d_w_query = exact_dot(target.T, d_query)
    spare = HID - LANES
    room = LANES - spare
    low = jnp.concatenate([d_w_query, jnp.zeros((E, LANES - E), F32)], axis=1)
    row_a = d_w_logit[:, 0:LANES]
    row_b = jnp.concatenate([d_w_logit[:, LANES:HID], jnp.zeros((1, room), F32)], axis=1)
    logit_rows = [
        pltpu.roll(row_a, spare, 1), pltpu.roll(row_a, spare - room, 1), pltpu.roll(row_a, spare + LANES - 2 * room, 1),
        pltpu.roll(row_b, spare, 1), pltpu.roll(row_b, spare - room, 1), jnp.zeros((E - 5, LANES), F32),
    ]
    extra = [pltpu.roll(low, spare, 1), pltpu.roll(low, spare - room, 1)] + logit_rows
    second = weights[:, LANES : 2 * LANES]
    free = iota((3 * E, LANES), 1) >= spare
    weights[:, LANES : 2 * LANES] = jnp.where(free, jnp.concatenate(extra, axis=0), second)

    @pl.loop(1, nr)
    def _(i):
        to = lax.rem(rep + i, nr)
        piece = weights.at[pl.ds(pl.multiple_of(to * PIECE, 8), PIECE)]
        send(piece, weights_z.at[i - 1], (wz_sem.at[0], wz_sem.at[1]), {"rep": to})

    drains.append((weights_z, wz_sem.at[0]))
    vectors = jnp.concatenate([d_pooled, query, d_target], axis=0)
    vectors = jnp.concatenate([vectors, jnp.zeros((3 * USERS, LANES - E), F32)], axis=1)
    vectors = jnp.concatenate([vectors, jnp.zeros((LANES - 3 * USERS, LANES), F32)], axis=0).T
    for i in range(3 * USERS):
        cast[i] = jnp.broadcast_to(vectors[0:E, i : i + 1], (E, LANES))

    def slot_grads(c):
        at = pl.ds(pl.multiple_of(c * LANES, LANES), LANES)
        w_c, s_c, n_c, a_c = weight[:, at], dscore[:, at], count[:, at], aimed[:, at]
        halves = []
        for h in range(2):
            acc = jnp.zeros((E, LANES), F32)
            for u in range(USERS):
                row = slice(h * USERS + u, h * USERS + u + 1)
                key_grad = w_c[row] * cast[u] + s_c[row] * cast[USERS + u]
                key_grad = key_grad.astype(BF16).astype(F32)
                acc = acc + n_c[row] * key_grad + a_c[row] * cast[2 * USERS + u]
            halves.append(acc)
        slot_grad[at, :] = jnp.concatenate(halves, axis=0).T

    def send_grads(to, landing, first_row, count_of, sems):
        src = slot_grad.at[pl.ds(pl.multiple_of(to * pairs + first_row, 8), count_of)]
        dst = landing.at[pl.ds(pl.multiple_of(me * count_of, 8), count_of)]

        @pl.when(to != me)
        def _():
            send(src, dst, sems, {"table": to})

        @pl.when(to == me)
        def _():
            pltpu.make_async_copy(src, dst, sems[1]).start()

    early = early_rows(pairs)
    late = pairs - early
    for g in (2, 1, 3, 0):
        group = lax.rem(my_group + g, groups)

        for i in range(group_chunks):
            slot_grads(group * group_chunks + i)
            low, high = i * LANES // pairs, (i + 1) * LANES // pairs

            @pl.loop(0, high - low)
            def _(m):
                to = group * members + low + lax.rem(me + m, high - low)
                send_grads(to, homed_a, 0, early, (grad_sem.at[0], grad_sem.at[1]))

    @pl.loop(0, nt)
    def _(j):
        send_grads(partner(j), homed_b, early, late, (grad_sem.at[2], grad_sem.at[3]))

    drains.append((homed_a.at[pl.ds(0, (nt - 1) * early)], grad_sem.at[0]))
    drains.append((homed_b.at[pl.ds(0, (nt - 1) * late)], grad_sem.at[2]))
    wait_bytes(weights_z, wz_sem.at[1])
    piece = weights[pl.ds(pl.multiple_of(rep * PIECE, 8), PIECE), :]
    for i in range(nr - 1):
        piece = piece + weights_z[i]
    def add_up(ref, count_of):
        out = ref[0]
        for i in range(1, count_of):
            out = out + ref[i]
        return out

    def send_cores():
        weights_c[core] = piece
        send(weights_c.at[core], weights_c.at[core], (wc_sem.at[0], wc_sem.at[1]), {"table": me + 1 - 2 * core})
        drains.append((weights_c.at[0], wc_sem.at[0]))

    def send_x():
        drains.append((weights_x.at[pl.ds(0, CHIPS_X - 1)], wx_sem.at[0]))
        wait_bytes(weights_c.at[0], wc_sem.at[1])
        weights_x[chip_x] = add_up(weights_c, CORES)

        @pl.loop(1, CHIPS_X)
        def _(i):
            to = lax.rem(chip_x + i, CHIPS_X)
            send(weights_x.at[chip_x], weights_x.at[chip_x], (wx_sem.at[0], wx_sem.at[1]),
                 {"table": (chip_y * CHIPS_X + to) * CORES + core})

    def send_y():
        drains.append((weights_y.at[pl.ds(0, chips_y - 1)], wy_sem.at[0]))
        wait_bytes(weights_x.at[pl.ds(0, CHIPS_X - 1)], wx_sem.at[1])
        weights_y[chip_y] = add_up(weights_x, CHIPS_X)

        @pl.loop(1, chips_y)
        def _(i):
            to = lax.rem(chip_y + i, chips_y)
            send(weights_y.at[chip_y], weights_y.at[chip_y], (wy_sem.at[0], wy_sem.at[1]),
                 {"table": (to * CHIPS_X + chip_x) * CORES + core})

    def send_weights():
        wait_bytes(weights_y.at[pl.ds(0, chips_y - 1)], wy_sem.at[1])
        total = add_up(weights_y, chips_y)
        for spot in range(row):
            cuts[spot] = total[spot * PIECE // row : (spot + 1) * PIECE // row]
        spread_out[rep] = cuts[lax.rem(me, row)]

        @pl.loop(1, nr)
        def _(i):
            to = lax.rem(rep + i, nr)
            send(spread_out.at[rep], spread_out.at[rep], (ws_sem.at[0], ws_sem.at[1]), {"rep": to})

        drains.append((spread_out.at[pl.ds(0, nr - 1)], ws_sem.at[0]))

    def share_weights():
        wait_bytes(spread_out.at[pl.ds(0, nr - 1)], ws_sem.at[1])
        spot = lax.rem(me, row)
        joined[spot] = spread_out[...]

        @pl.loop(1, row)
        def _(i):
            to = chip_y * row + lax.rem(spot + i, row)
            send(joined.at[spot], joined.at[spot], (wj_sem.at[0], wj_sem.at[1]), {"table": to})

        drains.append((joined.at[pl.ds(0, row - 1)], wj_sem.at[0]))

    def own(dest, k):
        at = k * nr + dest
        if k == 0:
            rows_of = homed_a[pl.ds(at, nt, stride=early), :]
        else:
            ahead = at < early
            in_a = homed_a[pl.ds(jnp.minimum(at, early - 1), nt, stride=early), :]
            in_b = homed_b[pl.ds(jnp.maximum(at - early, 0), nt, stride=late), :]
            rows_of = jnp.where(ahead, in_a, in_b)
        here = bf16_dot(onehot[at], jnp.concatenate(split3(rows_of), axis=1))
        here = here[:, 0:LANES] + here[:, LANES : 2 * LANES] + here[:, 2 * LANES : 3 * LANES]
        return jnp.where(low_half, here[0:E], here[E : 2 * E])

    strides = (2, 2)
    sign = (1 - 2 * core, 2 * core - 1)
    reaches = ((nr // 2, 1), (nr - 1 - nr // 2, -1))

    def plan_of(stride):
        stages = {}
        slot = {}
        for reach, way in reaches:
            for distance in range(reach, 0, -1):
                level = distance // stride if distance % stride == 0 and distance < reach else None
                slot[distance * way] = len(slot)
                terms = () if level is None else tuple(
                    slot[way * d] for d in range(distance + 1, min(distance + stride, reach) + 1)
                )
                hop = (distance - 1) % stride + 1
                stages.setdefault(level, []).append((slot[distance * way], distance * way, hop * way, terms))
        top = max(level for level in stages if level is not None)
        leaves = sorted(stages[None], key=lambda item: -abs(item[1]))
        last = tuple(slot[way * d] for reach, way in reaches for d in range(1, stride + 1))
        return [leaves] + [stages[level] for level in range(top, 0, -1)] + [[(None, 0, 0, last)]]

    plans = [plan_of(stride) for stride in strides]

    def sum_stage(k, stage):
        items_of = plans[k][stage]
        for start in range(0, len(items_of), 3):
            batch = items_of[start : start + 3]
            values = [own(at_rep(sign[k] * far), k) for _, far, _, _ in batch]
            for value, (slot, _, hop, terms) in zip(values, batch):
                for term in terms:
                    wait_bytes(got.at[term, k], rs_recv.at[term, k])
                    value = value + got[term, k]
                if slot is None:
                    return value
                sums[slot, k] = value
                send(sums.at[slot, k], got.at[slot, k], (rs_send.at[slot, k], rs_recv.at[slot, k]), {"rep": at_rep(sign[k] * hop)})
                drains.append((sums.at[slot, k], rs_send.at[slot, k]))

    def adagrad(k, value):
        turned = jnp.concatenate([value, jnp.zeros_like(value)], axis=0).T
        grads = jnp.where(low_half, turned[0:E], pltpu.roll(turned[E : 2 * E], E, 1))
        at = rep * per_rep + k
        new_accum = accum[at] + jnp.sum(grads * grads, axis=0, keepdims=True) * (1.0 / E)
        old = items[:, pl.ds(pl.multiple_of(at * LANES, LANES), LANES)]
        share[rep, k, 0:E, :] = old - LEARN_RATE * grads / jnp.sqrt(new_accum)
        accums[k : k + 1, :] = new_accum
        if k == per_rep - 1:
            share[rep, k, E : E + 8, :] = accums[...]

    def place(r, k):
        at = r * per_rep + k
        out_rows[:, pl.ds(pl.multiple_of(at * LANES, LANES), LANES)] = share[r, k, 0:E, :]
        if k == per_rep - 1:
            for i in range(per_rep):
                out_accum[r * per_rep + i] = share[r, k, E + i : E + i + 1, :]

    def block_of(r, k):
        return share.at[r, k, pl.ds(0, E + 8 * (k == per_rep - 1))]

    def share_stage(k, stage):
        stride = strides[k]
        for reach, way in reaches:
            side = 0 if way == 1 else nr // 2
            part = block_of(at_rep(-sign[k] * way * stride * stage), k)
            if stage and stride * stage < reach:
                wait_bytes(part, ag_recv.at[side + stride * stage - 1, k])
            for hop in range(stride, 0, -1):
                distance = stride * stage + hop
                if distance <= reach:
                    at = side + distance - 1
                    send(part, part, (ag_send.at[at, k], ag_recv.at[at, k]), {"rep": at_rep(sign[k] * way * hop)})
                    drains.append((part, ag_send.at[at, k]))

    def place_stage(k, stage):
        stride = strides[k]
        for hop in range(1, stride + 1):
            for reach, way in reaches:
                side = 0 if way == 1 else nr // 2
                distance = stride * stage + hop
                if distance <= reach:
                    source = at_rep(-sign[k] * way * distance)
                    if distance % stride or distance == reach:
                        wait_bytes(block_of(source, k), ag_recv.at[side + distance - 1, k])
                    place(source, k)

    send_cores()
    wait_bytes(homed_a, grad_sem.at[1])
    sum_stage(0, 0)
    sum_stage(0, 1)
    wait_bytes(homed_b, grad_sem.at[3])
    sum_stage(1, 0)
    send_x()
    sum_stage(0, 2)
    sum_stage(1, 1)
    send_y()
    adagrad(0, sum_stage(0, 3))
    share_stage(0, 0)
    sum_stage(1, 2)
    send_weights()
    place(rep, 0)
    share_stage(0, 1)
    adagrad(1, sum_stage(1, 3))
    share_stage(1, 0)
    share_weights()
    place(rep, 1)
    share_stage(0, 2)
    place_stage(0, 0)
    share_stage(1, 1)
    place_stage(0, 1)
    place_stage(1, 0)
    share_stage(1, 2)
    place_stage(0, 2)
    place_stage(1, 1)
    wait_bytes(joined.at[pl.ds(0, row - 1)], wj_sem.at[1])
    for spot in range(row):
        for r in range(nr):
            at = r * PIECE + spot * (PIECE // row)
            whole[at : at + PIECE // row, :] = joined[spot, r]
    flat = whole[...]
    out_hidden[...] = flat[:, 0:HID]
    second = flat[:, LANES : 2 * LANES]
    lane_e = iota((E, LANES), 1)
    query_grad = jnp.where(lane_e < room, pltpu.roll(second[0:E], room, 1), pltpu.roll(second[E : 2 * E], LANES - spare + room, 1))
    out_query[...] = query_grad[:, 0:E]
    tail = second[2 * E : 2 * E + 8]
    lane_1 = iota((1, LANES), 1)

    def turn(row, by):
        return pltpu.roll(tail, by, 1)[row : row + 1]

    row_a = jnp.where(lane_1 < room, turn(0, room), jnp.where(lane_1 < 2 * room, turn(1, 2 * room), turn(2, 2 * room - spare)))
    row_b = jnp.where(lane_1 < room, turn(3, room), turn(4, 2 * room))
    out_logit[:, 0:LANES] = row_a
    out_logit[:, LANES:HID] = row_b[:, 0 : HID - LANES]

    place_stage(1, 2)

    for ref, sem in drains:
        wait_bytes(ref, sem)


def finish(count_of, *refs):
    sem = refs[-1]
    copies = [pltpu.make_async_copy(refs[i], refs[count_of + i], sem.at[i]) for i in range(count_of)]
    for copy in copies:
        copy.start()
    for copy in copies:
        copy.wait()


def local(
    nt, nr, item_rows, row_accum, w_query, w_hidden, w_logit, wanted_rows, behaviour_slots,
    target_slots, seq_lengths, clicks, fake_flags,
):
    rows = item_rows.shape[0]
    capacity = wanted_rows.shape[2]
    pairs = capacity // 2
    columns = nt * pairs
    seq = behaviour_slots.shape[1]
    per_rep = pairs // nr
    vmem = pl.BlockSpec(memory_space=pltpu.VMEM)

    def in_hbm(x):
        return pltpu.with_memory_space_constraint(x, pltpu.HBM)

    hbm = pl.BlockSpec(memory_space=pltpu.HBM)
    dma = pltpu.SemaphoreType.DMA
    wide = 2 * LANES
    row = CORES * CHIPS_X
    scratch = [
        pltpu.VMEM((E, rows), F32),
        pltpu.VMEM((rows // LANES, 1, LANES), F32),
        pltpu.VMEM((E, E), F32),
        pltpu.VMEM((3 * E, HID), F32),
        pltpu.VMEM((1, HID), F32),
        pltpu.VMEM((capacity, nt), jnp.int32),
        pltpu.VMEM((USERS, seq), jnp.int32),
        pltpu.SMEM((USERS,), jnp.int32),
        pltpu.SMEM((USERS,), jnp.int32),
        pltpu.SMEM((USERS,), jnp.int32),
        pltpu.SMEM((USERS,), jnp.int32),
        pltpu.VMEM((3 * LANES, rows), BF16),
        pltpu.VMEM((nt, 1, LANES), jnp.int32),
        pltpu.VMEM((nt, 1, LANES), jnp.int32),
        pltpu.VMEM((pairs, LANES, nt), BF16),
        pltpu.VMEM((columns, LANES), F32),
        pltpu.VMEM((columns, LANES), F32),
        pltpu.VMEM((3, columns, LANES), BF16),
        pltpu.VMEM((2 * USERS, columns), F32),
        pltpu.VMEM((2 * USERS, columns), F32),
        pltpu.VMEM((USERS, 1, seq), jnp.int32),
        pltpu.VMEM((USERS, 1, seq), jnp.int32),
        pltpu.VMEM((2 * USERS, columns), F32),
        pltpu.VMEM((2 * USERS, columns), F32),
        pltpu.VMEM((3 * USERS, E, LANES), F32),
        pltpu.VMEM((columns, LANES), F32),
        pltpu.VMEM((nt * early_rows(pairs), LANES), F32),
        pltpu.VMEM((nt * (pairs - early_rows(pairs)), LANES), F32),
        pltpu.VMEM((LANES, 1, LANES), jnp.int32),
        pltpu.VMEM((USERS, 2 * columns // LANES, LANES), F32),
        pltpu.VMEM((nr - 1, per_rep, E, LANES), F32),
        pltpu.VMEM((nr - 1, per_rep, E, LANES), F32),
        pltpu.VMEM((nr * PIECE, wide), F32),
        pltpu.VMEM((nr - 1, PIECE, wide), F32),
        pltpu.VMEM((CORES, PIECE, wide), F32),
        pltpu.VMEM((CHIPS_X, PIECE, wide), F32),
        pltpu.VMEM((nt // (CORES * CHIPS_X), PIECE, wide), F32),
        pltpu.VMEM((row, PIECE // row, wide), F32),
        pltpu.VMEM((nr, PIECE // row, wide), F32),
        pltpu.VMEM((row, nr, PIECE // row, wide), F32),
        pltpu.VMEM((nr * PIECE, wide), F32),
        pltpu.VMEM((8, LANES), F32),
        pltpu.VMEM((nr, per_rep, E + 8, LANES), F32),
        dma((11,)), dma((2,)), dma((5,)), dma((4,)), dma((2,)), dma((2,)), dma((2,)), dma((2,)), dma((2,)), dma((2,)),
        dma((nr - 1, per_rep)), dma((nr - 1, per_rep)), dma((nr - 1, 2)), dma((nr - 1, 2)),
    ]
    results = pl.pallas_call(
        functools.partial(kernel, nt, nr, capacity),
        out_shape=(
            pltpu.VMEM((E, rows), F32),
            pltpu.VMEM((rows // LANES, 1, LANES), F32),
            pltpu.VMEM((E, E), F32),
            pltpu.VMEM((3 * E, HID), F32),
            pltpu.VMEM((1, HID), F32),
        ),
        in_specs=[hbm] * 11,
        out_specs=[vmem] * 5,
        scratch_shapes=scratch,
        compiler_params=pltpu.CompilerParams(
            collective_id=0, has_side_effects=True, vmem_limit_bytes=VMEM
        ),
    )(
        in_hbm(item_rows.T),
        in_hbm(row_accum.reshape(rows // LANES, 1, LANES)),
        in_hbm(w_query),
        in_hbm(w_hidden),
        in_hbm(w_logit.reshape(1, HID)),
        in_hbm(wanted_rows[0].T),
        in_hbm(behaviour_slots),
        in_hbm(target_slots),
        in_hbm(seq_lengths),
        in_hbm(clicks),
        in_hbm(fake_flags),
    )
    new_rows, new_accum, grad_query, grad_hidden, grad_logit = pl.pallas_call(
        functools.partial(finish, 5),
        out_shape=[jax.ShapeDtypeStruct(result.shape, result.dtype) for result in results],
        in_specs=[vmem] * 5,
        out_specs=[hbm] * 5,
        scratch_shapes=[dma((5,))],
        compiler_params=pltpu.CompilerParams(vmem_limit_bytes=VMEM),
    )(*[pltpu.with_memory_space_constraint(result, pltpu.VMEM) for result in results])
    return (new_rows.T, new_accum.reshape(rows), grad_query, grad_hidden, grad_logit.reshape(HID))


def solution(mesh):
    in_specs = (
        P("table", None),
        P("table"),
        P(),
        P(),
        P(),
        P(("table", "rep"), None, None),
        P(("table", "rep"), None),
        P(("table", "rep")),
        P(("table", "rep")),
        P(("table", "rep")),
        P(("table", "rep")),
    )
    out_specs = (P("table", None), P("table"), P(), P(), P())
    return jax.shard_map(
        functools.partial(local, mesh.shape["table"], mesh.shape["rep"]),
        mesh=mesh, in_specs=in_specs, out_specs=out_specs, check_vma=False,
    )
```
